256 devices in a mesh: lon: 32 (over z, y_hi, core), lat: 4 (over x), lev: 2 (over y_lo).
Axes of the slice: x: 4, y: 4 (y_hi: 2, y_lo: 2; y = y_hi * 2 + y_lo), z: 8, core: 2. Of those that a mesh axis runs over, the one named last changes fastest.
Arguments:
- fields: bfloat16 [2, 4, 48, 768, 192], P(None, 'lev', 'lat', 'lon'), may hold values from -6 to 6
- upstream: bfloat16 [2, 4, 48, 768, 192], P(None, 'lev', 'lat', 'lon'), may hold values from -6 to 6
- qkv_weight: bfloat16 [192, 576], replicated, may hold values from -0.4375 to 0.4375
- out_weight: bfloat16 [192, 192], replicated, may hold values from -0.4375 to 0.4375
- earth_bias: float32 [2, 8, 6, 3312], P('lev', 'lat'), may hold values from -6 to 260
Outputs:
- field_grad: float32 [2, 4, 48, 768, 192], P(None, 'lev', 'lat', 'lon')
- qkv_grad: float32 [192, 576], replicated
- out_grad: float32 [192, 192], replicated
- bias_grad: float32 [2, 8, 6, 3312], P('lev', 'lat')
The draws below stay inside these ranges and needn't reach their ends.
All inputs are finite; a program needn't handle non-finite values.
Results may differ from the reference program's by a relative error of at most 0.0085.
Values may be sent and summed in bfloat16 or wider, within the bound.
No kernel may reach another device: no remote copies, remote signals or barrier semaphores. Data moves between devices by JAX's collectives and lax.ppermute only.
A program may use at most 128 MiB of HBM per device.

```python
import math
import jax
import jax.numpy as jnp
from jax import lax

C = 192
HEADS = 6
WZ = 2
WH = 6
WW = 12
BATCH = 2
WIN = 144
PAIRS = 3312
NLEV = 4
NLAT = 48
NLON = 768
LEVWIN = 2
LATWIN = 8
TOTAL = 294912


def draw_earth_bias(key, part):
    key = jax.random.fold_in(key, 11)
    base_key = jax.random.fold_in(key, 0)
    groups = (LEVWIN, LATWIN, HEADS, WZ * WZ * WH * WH)
    drawn = jnp.clip(jax.random.normal(base_key, groups + (2 * WW - 1,), jnp.float32), -6.0, 6.0)
    return drawn.reshape(LEVWIN, LATWIN, HEADS, PAIRS)


def raised(result, stream_key, source, target, parts, factor):
    owner, partner = [(jnp.arange(result.shape[dim]) // (result.shape[dim] // parts)).reshape([-1 if axis == dim else 1 for axis in range(result.ndim)]) for dim in (source, target)]
    chosen = jax.random.permutation(stream_key, parts)[partner]
    strong = (owner == chosen) | (owner == (partner + parts // 2) % parts)
    return jnp.where(strong, factor * result, result)


def block_levels(rng, extent, pieces, least, high):
    def one(axis_at, shards_of):
        steps = jax.random.uniform(jax.random.fold_in(jax.random.fold_in(rng, 6), axis_at), (shards_of,), jnp.float32, least / len(pieces), high / len(pieces))
        return jnp.repeat(jnp.exp(steps), extent[axis_at] // shards_of).reshape((-1,) + (1,) * (len(extent) - axis_at - 1))

    gain = one(*pieces[0])
    for cut in pieces[1:]:
        gain = gain * one(*cut)
    return gain


def gaussian(rng, dims, width, reach, pieces=(), kind=jnp.bfloat16):
    values = jax.random.normal(rng, dims, jnp.float32) * width
    if len(pieces) > 0:
        values = block_levels(rng, dims, pieces, -0.22, 0.18) * values
    return jnp.clip(values, min=-reach, max=reach).astype(kind)


def bell_draw_with(stream_key, dims, scale, most, shards, heavy, kind=jnp.bfloat16):
    entries = scale * jax.random.normal(stream_key, dims, jnp.float32)
    if shards:
        entries = entries * block_levels(stream_key, dims, shards, -0.22, 0.18)
    return jnp.clip(raised(entries, jax.random.fold_in(stream_key, 3), *heavy), -most, most).astype(kind)


def setup_inputs(seed: int = 0) -> dict:
    key_list = jax.random.split(jax.random.key(seed), 6)
    fields = gaussian(key_list[0], (BATCH, NLEV, NLAT, NLON, C), 1.0, 6.0, ((1, 2), (2, 4), (3, 32)))
    upstream = bell_draw_with(key_list[1], (BATCH, NLEV, NLAT, NLON, C), 1.0, 6.0, ((1, 2), (2, 4), (3, 32)), (3, 4, 32, 2.75))
    qkv_weight = gaussian(key_list[2], (C, 3 * C), C ** -0.5, 0.4375)
    out_weight = gaussian(key_list[3], (C, C), C ** -0.5, 0.4375)
    earth_bias = draw_earth_bias(jax.random.fold_in(key_list[5], 71), 0)
    return {"fields": fields, "upstream": upstream, "qkv_weight": qkv_weight, "out_weight": out_weight, "earth_bias": earth_bias}


NEG_FILL = -1e+30
EPS = 1e-05

def offset_onehot():
    first_pos = jnp.arange(WW, dtype=jnp.int32)[:, None]
    second_pos = jnp.arange(WW, dtype=jnp.int32)[None, :]
    offset = (first_pos - second_pos + WW - 1).reshape(WW * WW)
    return (offset[:, None] == jnp.arange(2 * WW - 1, dtype=jnp.int32)[None, :]).astype(jnp.float32)

def expand_pairs(pair_table):
    leading = pair_table.shape[:-1]
    lead_count = len(leading)
    gridded = pair_table.reshape(leading + (WZ, WZ, WH, WH, 2 * WW - 1))
    spread = jnp.dot(gridded, offset_onehot().T, precision=lax.Precision.HIGHEST)
    spread = spread.reshape(leading + (WZ, WZ, WH, WH, WW, WW))
    axes_order = tuple(range(lead_count)) + tuple((lead_count + position for position in (0, 2, 4, 1, 3, 5)))
    return spread.transpose(axes_order).reshape(leading + (WIN, WIN))

def fold_pairs(score_grads):
    leading = score_grads.shape[:-2]
    lead_count = len(leading)
    unfolded = score_grads.reshape(leading + (WZ, WH, WW, WZ, WH, WW))
    axes_order = tuple(range(lead_count)) + tuple((lead_count + position for position in (0, 3, 1, 4, 2, 5)))
    unfolded = unfolded.transpose(axes_order).reshape(leading + (WZ, WZ, WH, WH, WW * WW))
    folded = jnp.dot(unfolded, offset_onehot(), precision=lax.Precision.HIGHEST)
    return folded.reshape(leading + (PAIRS,))

def window_backward(raw_tokens, up_tokens, bias_full, allowed, qkv_weight, out_weight):
    windows_n, window_len, channels = raw_tokens.shape
    head_size = channels // HEADS
    scaling = head_size ** (-0.5)
    widened = raw_tokens.astype(jnp.float32)
    average = lax.optimization_barrier(jnp.mean(widened, axis=-1, keepdims=True))
    centred = widened - average
    inv_std = lax.rsqrt(lax.optimization_barrier(jnp.mean(centred * centred, axis=-1, keepdims=True)) + EPS)
    normed = centred * inv_std
    normed_low = normed.astype(jnp.bfloat16).reshape(windows_n * window_len, channels)
    packed = jnp.dot(normed_low, qkv_weight, preferred_element_type=jnp.float32).astype(jnp.bfloat16)
    packed = packed.reshape(windows_n, window_len, 3, HEADS, head_size).transpose(2, 0, 3, 1, 4)
    query_heads = packed[0].astype(jnp.float32)
    key_heads = packed[1].astype(jnp.float32)
    value_heads = packed[2].astype(jnp.float32)
    scores = jnp.einsum('nhqd,nhkd->nhqk', query_heads, key_heads) * scaling + bias_full
    scores = jnp.where(allowed[:, None], scores, NEG_FILL)
    highest = lax.optimization_barrier(jnp.max(scores, axis=-1, keepdims=True))
    expos = jnp.exp(scores - highest)
    attn_probs = expos / lax.optimization_barrier(jnp.sum(expos, axis=-1, keepdims=True))
    probs_low = attn_probs.astype(jnp.bfloat16)
    attended = jnp.einsum('nhqk,nhkd->nhqd', probs_low.astype(jnp.float32), value_heads).astype(jnp.bfloat16)
    attended = attended.transpose(0, 2, 1, 3).reshape(windows_n * window_len, channels)
    up_rows = up_tokens.reshape(windows_n * window_len, channels)
    out_part = jnp.dot(attended.T, up_rows, preferred_element_type=jnp.float32)
    grad_att = jnp.dot(up_rows, out_weight.T, preferred_element_type=jnp.float32).astype(jnp.bfloat16)
    grad_att = grad_att.reshape(windows_n, window_len, HEADS, head_size).transpose(0, 2, 1, 3).astype(jnp.float32)
    grad_probs = jnp.einsum('nhqd,nhkd->nhqk', grad_att, value_heads)
    grad_values = jnp.einsum('nhqk,nhqd->nhkd', probs_low.astype(jnp.float32), grad_att)
    inner_sum = lax.optimization_barrier(jnp.sum(attn_probs * grad_probs, axis=-1, keepdims=True))
    grad_scores = attn_probs * (grad_probs - inner_sum)
    scores_low = grad_scores.astype(jnp.bfloat16).astype(jnp.float32)
    grad_queries = jnp.einsum('nhqk,nhkd->nhqd', scores_low, key_heads) * scaling
    grad_keys = jnp.einsum('nhqk,nhqd->nhkd', scores_low, query_heads) * scaling
    grad_packed = jnp.stack([grad_queries, grad_keys, grad_values], axis=0).astype(jnp.bfloat16)
    grad_packed = grad_packed.transpose(1, 3, 0, 2, 4).reshape(windows_n * window_len, 3 * channels)
    qkv_part = jnp.dot(normed_low.T, grad_packed, preferred_element_type=jnp.float32)
    grad_units = jnp.dot(grad_packed, qkv_weight.T, preferred_element_type=jnp.float32)
    grad_units = grad_units.reshape(windows_n, window_len, channels)
    centre_grad = lax.optimization_barrier(jnp.mean(grad_units, axis=-1, keepdims=True))
    along_normed = lax.optimization_barrier(jnp.mean(grad_units * normed, axis=-1, keepdims=True))
    grad_raw = inv_std * (grad_units - centre_grad - normed * along_normed)
    return (grad_raw, qkv_part, out_part, grad_scores)

def reference(fields, upstream, qkv_weight, out_weight, earth_bias):
    shifts = (-(WZ // 2), -(WH // 2), -(WW // 2))
    lon_windows = NLON // WW

    def to_windows(volume):
        volume = volume.reshape(BATCH, LEVWIN, WZ, LATWIN, WH, lon_windows, WW, C)
        volume = volume.transpose(0, 1, 3, 5, 2, 4, 6, 7)
        return volume.reshape(BATCH * LEVWIN * LATWIN, lon_windows, WIN, C)
    raw_blocks = to_windows(jnp.roll(fields, shifts, axis=(1, 2, 3)))
    up_blocks = to_windows(jnp.roll(upstream, shifts, axis=(1, 2, 3)))
    block_ids = jnp.arange(BATCH * LEVWIN * LATWIN, dtype=jnp.int32)

    def per_block(carry, inputs_now):
        raw_block, up_block, block_id = inputs_now
        lat_win = block_id % LATWIN
        lev_win = block_id // LATWIN % LEVWIN
        lev_flag = (lev_win * WZ + jnp.arange(WZ, dtype=jnp.int32) >= NLEV - WZ // 2).astype(jnp.int32)
        lat_flag = (lat_win * WH + jnp.arange(WH, dtype=jnp.int32) >= NLAT - WH // 2).astype(jnp.int32)
        region = jnp.broadcast_to(2 * lev_flag[:, None, None] + lat_flag[None, :, None], (WZ, WH, WW)).reshape(WIN)
        allowed = region[:, None] == region[None, :]
        bias_full = expand_pairs(earth_bias[lev_win, lat_win])
        grad_raw, qkv_part, out_part, grad_scores = window_backward(raw_block, up_block, bias_full[None], allowed[None], qkv_weight, out_weight)
        pair_grad = fold_pairs(lax.optimization_barrier(jnp.sum(grad_scores, axis=0)))
        bias_acc = carry[2].at[lev_win, lat_win].add(pair_grad)
        return ((carry[0] + qkv_part, carry[1] + out_part, bias_acc), grad_raw)
    start = (jnp.zeros((C, 3 * C), jnp.float32), jnp.zeros((C, C), jnp.float32), jnp.zeros((LEVWIN, LATWIN, HEADS, PAIRS), jnp.float32))
    totals, grad_blocks = lax.scan(per_block, start, (raw_blocks, up_blocks, block_ids))
    grad_volume = grad_blocks.reshape(BATCH, LEVWIN, LATWIN, lon_windows, WZ, WH, WW, C)
    grad_volume = grad_volume.transpose(0, 1, 4, 2, 5, 3, 6, 7).reshape(BATCH, NLEV, NLAT, NLON, C)
    field_grad = jnp.roll(grad_volume, (WZ // 2, WH // 2, WW // 2), axis=(1, 2, 3))
    factor = 1.0 / math.sqrt(TOTAL)
    return (field_grad, totals[0] * factor, totals[1] * factor, totals[2])
```

```python
import functools
import math

import jax
import jax.numpy as jnp
from jax import lax
from jax.experimental import pallas as pl
from jax.experimental.pallas import tpu as pltpu
from jax.sharding import PartitionSpec as P

HEADS = 6
WZ = 2
WH = 6
WW = 12
WIN = 144
PAIRS = 3312
C = 192
HD = 32
OFFS = 2 * WW - 1
GROUP = WH * OFFS
LANES = 384
KEYS = 256
NEG_FILL = -1e30
EPS = 1e-05
SCALE = HD**-0.5
SLAB = 1536
WROWS = 1152
BF = jnp.bfloat16
F32 = jnp.float32
CHUNK = 48
VMEM = pl.BlockSpec(memory_space=pltpu.VMEM)
HBM = pl.BlockSpec(memory_space=pl.ANY)


def params(mib):
    return pltpu.CompilerParams(vmem_limit_bytes=mib * 1024 * 1024)


def cost(flops, nbytes):
    return pl.CostEstimate(flops=flops, bytes_accessed=nbytes, transcendentals=0)


def dot(a, b, ca=1, cb=0):
    return lax.dot_general(a, b, (((ca,), (cb,)), ((), ())), preferred_element_type=F32)


def shape(dims, dtype):
    return jax.ShapeDtypeStruct(dims, dtype)


def pack_first_kernel(f, u, lev, lat, diag):
    for t, src in enumerate((f, u)):
        for b in range(2):
            for r in range(9):
                lev[t, b, r] = src[b, 0, r + 3]
            for r in range(3):
                lat[t, b, r] = src[b, 1, r]
                diag[t, b, r] = src[b, 0, r]


def pack_first(fields, upstream):
    return pl.pallas_call(
        pack_first_kernel,
        name="pack_first",
        out_shape=(
            shape((2, 2, 9, 24, C), BF),
            shape((2, 2, 3, 24, C), BF),
            shape((2, 2, 3, 24, C), BF),
        ),
        in_specs=[VMEM] * 2,
        out_specs=(VMEM,) * 3,
        compiler_params=params(32),
        cost_estimate=cost(0, 2 * 1024 * 1024),
    )(fields, upstream)


def source_line(own, lev, lat, diag, t, b, z, r):
    if z == 0:
        return own[b, 1, r + 3] if r < 9 else lat[t, b, r - 9]
    return lev[t, b, r] if r < 9 else diag[t, b, r - 9]


def pack_lon_kernel(f, u, lev, lat, diag, out, tmp):
    for t, own in enumerate((f, u)):
        for b in range(2):
            for z in range(2):
                for r in range(12):
                    line = source_line(own, lev, lat, diag, t, b, z, r)
                    row = (t * 2 + b) * WIN + (z * 12 + r) * 6
                    tmp[row : row + 6, :] = line.astype(F32)[0:6]
    out[...] = tmp[...].astype(BF)


def pack_lon(fields, upstream, lev, lat, diag):
    return pl.pallas_call(
        pack_lon_kernel,
        name="pack_lon",
        out_shape=shape((4 * WIN, C), BF),
        in_specs=[VMEM] * 5,
        out_specs=VMEM,
        scratch_shapes=[pltpu.VMEM((4 * WIN, C), F32)],
        compiler_params=params(32),
        cost_estimate=cost(0, 2 * 1024 * 1024),
    )(fields, upstream, lev, lat, diag)


def onehot_rows(target, w1):
    lane = lax.broadcasted_iota(jnp.int32, (LANES, KEYS), 0)
    return jnp.where(lane == target + w1, 1.0, 0.0).astype(BF)


def expand_kernel(eb, target, rq, rk, out_a, out_b, spread):
    spread[...] = jnp.zeros_like(spread)
    for z1 in range(2):
        for h1 in range(6):
            g = z1 * 6 + h1
            for z2 in range(2):
                off = ((z1 * 2 + z2) * 6 + h1) * GROUP
                for aw in range(2):
                    spread[g * 16 + aw * 6 : g * 16 + aw * 6 + 6, z2 * GROUP : (z2 + 1) * GROUP] = eb[
                        0, aw, :, off : off + GROUP
                    ]
    full = spread[...]
    high = full.astype(BF)
    rest = full - high.astype(F32)
    mid = rest.astype(BF)
    low = (rest - mid.astype(F32)).astype(BF)
    row = lax.broadcasted_iota(jnp.int32, (12, 1), 0)
    tgt = target[...]
    for w1 in range(WW):
        hot = onehot_rows(tgt, w1)
        block = dot(high, hot) + (dot(mid, hot) + dot(low, hot))
        for g in range(12):
            q = g * 12 + w1
            part = block[g * 16 : g * 16 + 12]
            ok0 = rq[0, q : q + 1, :] == rk[0]
            ok1 = rq[1, q : q + 1, :] == rk[1]
            ok = ((row < 6) & ok0) | ((row >= 6) & ok1)
            part = jnp.where(ok, part, NEG_FILL)
            out_a[pl.ds(q, 12, stride=WIN), :] = part[:, 0:128]
            out_b[pl.ds(q, 12, stride=WIN), :] = part[:, 128:256]


def expand(earth_bias, target, rq, rk):
    return pl.pallas_call(
        expand_kernel,
        name="expand_bias",
        out_shape=(shape((12 * WIN, 128), F32),) * 2,
        in_specs=[VMEM] * 4,
        out_specs=(VMEM, VMEM),
        scratch_shapes=[pltpu.VMEM((192, LANES), F32)],
        compiler_params=params(32),
        cost_estimate=cost(12 * 3 * 2 * 192 * LANES * WIN, 4 * 1024 * 1024),
    )(earth_bias, target, rq, rk)


def main_kernel(
    f, u, lev, lat, diag, lon, wq, wk, wv, wo, bias_a, bias_b, target,
    lines, lon_back, slab,
    x_s, u_s, g_s, gb_a, gb_b, s_s, gp_s, p_s, gs_s, w_s, lon_s, spread,
):
    for t, (own, dst) in enumerate(((f, x_s), (u, u_s))):
        for b in range(2):
            halo = lon[(t * 2 + b) * WIN : (t * 2 + b + 1) * WIN, :].astype(F32)
            for z in range(2):
                for r in range(12):
                    line = source_line(own, lev, lat, diag, t, b, z, r).astype(F32)
                    w = (r // 6) * 4 + b * 2
                    off = z * 72 + (r % 6) * 12
                    hrow = (z * 12 + r) * 6
                    dst[w, off : off + 12, :] = line[6:18]
                    dst[w + 1, off : off + 6, :] = line[18:24]
                    dst[w + 1, off + 6 : off + 12, :] = halo[hrow : hrow + 6]
    gb_a[...] = jnp.zeros_like(gb_a)
    gb_b[...] = jnp.zeros_like(gb_b)
    w_s[...] = jnp.zeros_like(w_s)
    lane = lax.broadcasted_iota(jnp.int32, (1, C), 1)
    picks = [(lane >= h * HD) & (lane < (h + 1) * HD) for h in range(HEADS)]
    picks_low = [jnp.where(m, 1.0, 0.0).astype(BF) for m in picks]
    picks_f = [jnp.where(m, 1.0, 0.0) for m in picks]

    def stack(a):
        return jnp.concatenate([a * m for m in picks_low], axis=0)

    def unstack(a):
        total = a[0:WIN] * picks_f[0]
        for h in range(1, HEADS):
            total = total + a[h * WIN : (h + 1) * WIN] * picks_f[h]
        return total

    def window(w, carry):
        start = pl.multiple_of((w // 4) * (HEADS * WIN), HEADS * WIN)
        raw = x_s[w]
        centred = raw - jnp.mean(raw, axis=-1, keepdims=True)
        inv_std = lax.rsqrt(jnp.mean(centred * centred, axis=-1, keepdims=True) + EPS)
        normed = centred * inv_std
        low = normed.astype(BF)
        q = dot(low, wq[...]).astype(BF)
        k = dot(low, wk[...]).astype(BF)
        v = dot(low, wv[...]).astype(BF)
        up = u_s[w].astype(BF)
        ga = dot(up, wo[...], 1, 1).astype(BF)
        qs = stack(q)
        gas = stack(ga)
        s_s[...] = dot(qs, k, 1, 1)
        gp_s[...] = dot(gas, v, 1, 1)
        for i in range(HEADS * WIN // CHUNK):
            rows = slice(i * CHUNK, (i + 1) * CHUNK)
            brows = pl.ds(pl.multiple_of(start + i * CHUNK, CHUNK), CHUNK)
            both = jnp.concatenate([bias_a[brows, :], bias_b[brows, 0:16]], axis=1)
            s = s_s[rows, :] * SCALE + both
            e = jnp.exp(s - jnp.max(s, axis=-1, keepdims=True))
            p = e * (1.0 / jnp.sum(e, axis=-1, keepdims=True))
            gp = gp_s[rows, :]
            gs = p * (gp - jnp.sum(p * gp, axis=-1, keepdims=True))
            p_s[rows, :] = p.astype(BF)
            gs_s[rows, :] = gs.astype(BF)
            gb_a[brows, :] += gs[:, 0:128]
            gb_b[brows, 0:16] += gs[:, 128:144]
        p = p_s[...]
        gs = gs_s[...]
        att = unstack(dot(p, v)).astype(BF)
        gv = dot(p, gas, 0, 0).astype(BF)
        gq = (unstack(dot(gs, k)) * SCALE).astype(BF)
        gk = (dot(gs, qs, 0, 0) * SCALE).astype(BF)
        w_s[0:C, :] += dot(low, gq, 0, 0)
        w_s[C : 2 * C, :] += dot(low, gk, 0, 0)
        w_s[2 * C : 3 * C, :] += dot(low, gv, 0, 0)
        w_s[3 * C : 4 * C, :] += dot(att, up, 0, 0)
        gu = dot(gq, wq[...], 1, 1) + dot(gk, wk[...], 1, 1) + dot(gv, wv[...], 1, 1)
        centre = jnp.mean(gu, axis=-1, keepdims=True)
        along = jnp.mean(gu * normed, axis=-1, keepdims=True)
        g_s[w] = inv_std * (gu - centre - normed * along)
        return carry

    lax.fori_loop(0, 8, window, 0)

    for b in range(2):
        for z in range(2):
            for r in range(12):
                w = (r // 6) * 4 + b * 2
                off = z * 72 + (r % 6) * 12
                row = b * WIN + (z * 12 + r) * 6
                second = g_s[w + 1, off : off + 12, :]
                line = jnp.concatenate(
                    [jnp.zeros((6, C), F32), g_s[w, off : off + 12, :], second[0:6]], axis=0
                )
                lines[b, z, r] = line.astype(BF)
                lon_s[row : row + 6, :] = second[6:12]
    lon_back[...] = lon_s[...].astype(BF)

    slab[0:768, :] = w_s[:, 0:128].astype(BF)
    slab[768:1152, :] = jnp.concatenate([w_s[0:384, 128:192], w_s[384:768, 128:192]], axis=1).astype(BF)
    folded = jnp.zeros((192, LANES), F32)
    tgt = target[...]
    for w1 in range(WW):
        for g in range(12):
            picked = pl.ds(g * 12 + w1, 12, stride=WIN)
            spread[g * 16 : g * 16 + 12, 0:128] = gb_a[picked, :]
            spread[g * 16 : g * 16 + 12, 128:256] = gb_b[picked, :]
        full = spread[...]
        high = full.astype(BF)
        mid = (full - high.astype(F32)).astype(BF)
        hot = onehot_rows(tgt, w1)
        folded = folded + (dot(high, hot, 1, 1) + dot(mid, hot, 1, 1))
    tight = jnp.concatenate([folded[g * 16 : g * 16 + 12] for g in range(12)], axis=0)
    slab[1152:1296, :] = tight[:, 0:128].astype(BF)
    slab[1296:1440, :] = tight[:, 128:256].astype(BF)
    rest = [tight[24 * i : 24 * i + 24, 256:276] for i in range(6)]
    rest = jnp.concatenate(rest + [jnp.zeros((24, 8), F32)], axis=1)
    slab[1440:1536, :] = jnp.concatenate([rest, jnp.zeros((72, 128), F32)], axis=0).astype(BF)


def windows(fields, upstream, lev, lat, diag, lon, wq, wk, wv, wo, bias_a, bias_b, target):
    return pl.pallas_call(
        main_kernel,
        name="windows",
        out_shape=(
            shape((2, 2, 12, 24, C), BF),
            shape((2 * WIN, C), BF),
            shape((SLAB, 128), BF),
        ),
        in_specs=[VMEM] * 13,
        out_specs=(VMEM, VMEM, VMEM),
        scratch_shapes=[
            pltpu.VMEM((8, WIN, C), F32),
            pltpu.VMEM((8, WIN, C), F32),
            pltpu.VMEM((8, WIN, C), F32),
            pltpu.VMEM((12 * WIN, 128), F32),
            pltpu.VMEM((12 * WIN, 128), F32),
            pltpu.VMEM((HEADS * WIN, WIN), F32),
            pltpu.VMEM((HEADS * WIN, WIN), F32),
            pltpu.VMEM((HEADS * WIN, WIN), BF),
            pltpu.VMEM((HEADS * WIN, WIN), BF),
            pltpu.VMEM((4 * C, C), F32),
            pltpu.VMEM((2 * WIN, C), F32),
            pltpu.VMEM((192, KEYS), F32),
        ],
        compiler_params=params(48),
        cost_estimate=cost(2 * 10**9, 8 * 1024 * 1024),
    )(fields, upstream, lev, lat, diag, lon, wq, wk, wv, wo, bias_a, bias_b, target)


def merge_kernel(lines, lon_in, own, lev, lat, diag):
    for b in range(2):
        halo = lon_in[b * WIN : (b + 1) * WIN, :].astype(F32)
        for z in range(2):
            for r in range(12):
                row = (z * 12 + r) * 6
                line = jnp.concatenate(
                    [halo[row : row + 6], lines[b, z, r].astype(F32)[6:24]], axis=0
                ).astype(BF)
                if z == 0:
                    if r < 9:
                        own[b, r] = line
                    else:
                        lat[b, r - 9] = line
                elif r < 9:
                    lev[b, r] = line
                else:
                    diag[b, r - 9] = line


def merge(lines, lon_in):
    return pl.pallas_call(
        merge_kernel,
        name="merge_lon",
        out_shape=(
            shape((2, 9, 24, C), BF),
            shape((2, 9, 24, C), BF),
            shape((2, 3, 24, C), BF),
            shape((2, 3, 24, C), BF),
        ),
        in_specs=[VMEM] * 2,
        out_specs=(VMEM,) * 4,
        compiler_params=params(32),
        cost_estimate=cost(2 * 10**10, 2 * 1024 * 1024),
    )(lines, lon_in)


def place_kernel(own, lev, lat, diag, out):
    for b in range(2):
        out[b, 1, 3:12] = own[b].astype(F32)
        out[b, 1, 0:3] = lat[b].astype(F32)
        out[b, 0, 3:12] = lev[b].astype(F32)
        out[b, 0, 0:3] = diag[b].astype(F32)


def place(own, lev, lat, diag):
    return pl.pallas_call(
        place_kernel,
        name="place_grad",
        out_shape=shape((2, 2, 12, 24, C), F32),
        in_specs=[VMEM] * 4,
        out_specs=VMEM,
        compiler_params=params(32),
        cost_estimate=cost(2 * 10**10, 2 * 1024 * 1024),
    )(own, lev, lat, diag)


def finish_kernel(factor, slab, qkv, out, bias):
    full = slab[...].astype(F32)
    right = full[768:1152]
    rest = jnp.concatenate([right[:, 0:64], right[:, 64:128]], axis=0)
    whole = jnp.concatenate([full[0:768], rest], axis=1) * factor
    for j in range(3):
        qkv[:, j * C : (j + 1) * C] = whole[j * C : (j + 1) * C]
    out[...] = whole[3 * C : 4 * C]
    tail = full[1440:1464]
    tail = jnp.concatenate([tail[:, 20 * i : 20 * i + 20] for i in range(6)], axis=0)
    pairs = jnp.concatenate([full[1152:1296], full[1296:1440], tail], axis=1)
    for z1 in range(2):
        for h1 in range(6):
            g = z1 * 6 + h1
            for z2 in range(2):
                off = ((z1 * 2 + z2) * 6 + h1) * GROUP
                for aw in range(2):
                    bias[0, aw, :, off : off + GROUP] = pairs[
                        g * 12 + aw * 6 : g * 12 + aw * 6 + 6, z2 * GROUP : (z2 + 1) * GROUP
                    ]


def finish(slab, factor):
    return pl.pallas_call(
        functools.partial(finish_kernel, factor),
        name="finish_params",
        out_shape=(
            shape((C, 3 * C), F32),
            shape((C, C), F32),
            shape((1, 2, HEADS, PAIRS), F32),
        ),
        in_specs=[VMEM],
        out_specs=(VMEM,) * 3,
        compiler_params=params(32),
        cost_estimate=cost(0, 2 * 1024 * 1024),
    )(slab)


def from_behind(x, axis, by):
    devices = lax.axis_size(axis)
    return lax.ppermute(x, axis, [(i, (i + by) % devices) for i in range(devices)])


def from_corner(x, by):
    lats, levs = lax.axis_size("lat"), lax.axis_size("lev")
    pairs = [
        (a * levs + v, ((a + by) % lats) * levs + (v + by) % levs)
        for a in range(lats)
        for v in range(levs)
    ]
    return lax.ppermute(x, ("lat", "lev"), pairs)


def reduce_slab(slab):
    lons = lax.axis_size("lon")
    others = lax.axis_size("lat") * lax.axis_size("lev")
    rows = SLAB // lons
    pieces = lax.all_to_all(slab.reshape(lons, rows, 128), "lon", 0, 0, tiled=True)
    mine = jnp.sum(pieces.astype(F32), axis=0).astype(BF)
    every = lax.all_to_all(
        jnp.broadcast_to(mine[None], (others, rows, 128)), ("lat", "lev"), 0, 0, tiled=True
    )
    total = jnp.sum(every.astype(F32), axis=0).astype(BF)
    mine = jnp.where(lax.axis_index("lon") * rows < WROWS, total, mine)
    full = lax.all_to_all(jnp.broadcast_to(mine[None], (lons, rows, 128)), "lon", 0, 0, tiled=True)
    return full.reshape(SLAB, 128)


def body(fields, upstream, qkv_weight, out_weight, earth_bias):
    lev_msg, lat_msg, diag_msg = pack_first(fields, upstream)
    lev = from_behind(lev_msg, "lev", -1)
    lat = from_behind(lat_msg, "lat", -1)
    diag = from_corner(diag_msg, -1)

    key = jnp.arange(WIN, dtype=jnp.int32)
    target = (key // WW) * OFFS - key % WW + WW - 1
    target = jnp.concatenate([target, jnp.full((KEYS - WIN,), -1000, jnp.int32)])[None, :]
    last_lev = lax.axis_index("lev") == lax.axis_size("lev") - 1
    last_lat = lax.axis_index("lat") == lax.axis_size("lat") - 1
    lev_flag = ((key // 72) == 1) & last_lev
    lat_flag = ((key // WW) % WH >= WH // 2) & last_lat
    region = jnp.stack(
        [2 * lev_flag.astype(F32), 2 * lev_flag.astype(F32) + lat_flag.astype(F32)]
    )
    keys = jnp.concatenate([region, jnp.zeros((2, KEYS - WIN), F32)], axis=1)
    bias_a, bias_b = expand(earth_bias, target, region[:, :, None], keys[:, None, :])

    lon = from_behind(pack_lon(fields, upstream, lev, lat, diag), "lon", -1)
    lines, lon_back, slab = windows(
        fields, upstream, lev, lat, diag, lon,
        qkv_weight[:, 0:C], qkv_weight[:, C : 2 * C], qkv_weight[:, 2 * C :], out_weight,
        bias_a, bias_b, target,
    )
    lon_in = from_behind(lon_back, "lon", 1)
    own, lev_out, lat_out, diag_out = merge(lines, lon_in)
    lev_in = from_behind(lev_out, "lev", 1)
    lat_in = from_behind(lat_out, "lat", 1)
    diag_in = from_corner(diag_out, 1)
    field_grad = place(own, lev_in, lat_in, diag_in)

    samples, levels, rows, cols, _ = fields.shape
    tokens = samples * levels * rows * cols
    for axis in ("lon", "lat", "lev"):
        tokens = tokens * lax.axis_size(axis)
    qkv_grad, out_grad, bias_grad = finish(reduce_slab(slab), 1.0 / math.sqrt(tokens))
    return (field_grad, qkv_grad, out_grad, bias_grad)


def solution(mesh):
    return jax.shard_map(
        body,
        mesh=mesh,
        in_specs=(
            P(None, "lev", "lat", "lon", None),
            P(None, "lev", "lat", "lon", None),
            P(),
            P(),
            P("lev", "lat", None, None),
        ),
        out_specs=(P(None, "lev", "lat", "lon", None), P(), P(), P("lev", "lat", None, None)),
        check_vma=False,
    )
```

```python
import functools
import math

import jax
import jax.numpy as jnp
from jax import lax
from jax.experimental import pallas as pl
from jax.experimental.pallas import tpu as pltpu
from jax.sharding import PartitionSpec as P

HEADS = 6
WZ = 2
WH = 6
WW = 12
WIN = 144
PAIRS = 3312
C = 192
HD = 32
OFFS = 2 * WW - 1
GROUP = WH * OFFS
LANES = 384
KEYS = 256
NEG_FILL = -1e30
EPS = 1e-05
SCALE = HD**-0.5
SLAB = 1536
SIDE = SLAB // 2
WROWS = 1152
BF = jnp.bfloat16
F32 = jnp.float32
SPREAD = 896
PAIR = 2 * WIN
BOTH = 2 * C
VMEM = pl.BlockSpec(memory_space=pltpu.VMEM)
HBM = pl.BlockSpec(memory_space=pl.ANY)
SMEM = pl.BlockSpec(memory_space=pltpu.SMEM)


def params(mib):
    return pltpu.CompilerParams(vmem_limit_bytes=mib * 1024 * 1024)


def cost(flops, nbytes):
    return pl.CostEstimate(flops=flops, bytes_accessed=nbytes, transcendentals=0)


def dot(a, b, ca=1, cb=0):
    return lax.dot_general(a, b, (((ca,), (cb,)), ((), ())), preferred_element_type=F32)


def shape(dims, dtype):
    return jax.ShapeDtypeStruct(dims, dtype)


def join(a, b):
    return jnp.concatenate([a[:, 0:128], b[:, 0:128], a[:, 128:C], b[:, 128:C]], axis=1)


def split(m):
    return (
        jnp.concatenate([m[:, 0:128], m[:, 256:320]], axis=1),
        jnp.concatenate([m[:, 128:256], m[:, 320:384]], axis=1),
    )


def pack_near_kernel(f, u, near):
    for b in range(2):
        for h in range(6):
            near[b, h] = join(f[b, 0, h + 3], u[b, 0, h + 3])


def pack_near(fields, upstream):
    return pl.pallas_call(
        pack_near_kernel,
        name="pack_near",
        out_shape=shape((2, 6, 24, BOTH), BF),
        in_specs=[VMEM] * 2,
        out_specs=VMEM,
        compiler_params=params(16),
        cost_estimate=cost(0, 2 * 1024 * 1024),
    )(fields, upstream)


def pack_rest_kernel(f, u, far, lat, diag):
    for b in range(2):
        for r in range(3):
            far[b, r] = join(f[b, 0, r + 9], u[b, 0, r + 9])
            lat[b, r] = join(f[b, 1, r], u[b, 1, r])
            diag[b, r] = join(f[b, 0, r], u[b, 0, r])


def pack_rest(fields, upstream):
    return pl.pallas_call(
        pack_rest_kernel,
        name="pack_rest",
        out_shape=(shape((2, 3, 24, BOTH), BF),) * 3,
        in_specs=[VMEM] * 2,
        out_specs=(VMEM,) * 3,
        compiler_params=params(16),
        cost_estimate=cost(0, 2 * 1024 * 1024),
    )(fields, upstream)


def source_lines(own, halos, aw, b, z, h):
    if z == 0 and (aw == 0 or h < 3):
        return [a[b, 1, 6 * aw + h + 3].astype(F32) for a in own]
    if aw == 0:
        line = halos[0][b, h]
    elif z == 0:
        line = halos[2][b, h - 3]
    else:
        line = halos[1][b, h] if h < 3 else halos[3][b, h - 3]
    return split(line.astype(F32))


def pack_lon_kernel(f, u, near, far, lat, diag, out, tmp):
    for b in range(2):
        for z in range(2):
            for r in range(12):
                lines = source_lines((f, u), (near, far, lat, diag), r // 6, b, z, r % 6)
                row = b * WIN + (z * 12 + r) * 6
                tmp[row : row + 6, :] = join(lines[0][0:6], lines[1][0:6])
    out[...] = tmp[...].astype(BF)


def pack_lon(fields, upstream, halos):
    return pl.pallas_call(
        pack_lon_kernel,
        name="pack_lon",
        out_shape=shape((2 * WIN, BOTH), BF),
        in_specs=[VMEM] * 6,
        out_specs=VMEM,
        scratch_shapes=[pltpu.VMEM((2 * WIN, BOTH), F32)],
        compiler_params=params(16),
        cost_estimate=cost(0, 2 * 1024 * 1024),
    )(fields, upstream, *halos)


def onehot_rows(target, w1):
    lane = lax.broadcasted_iota(jnp.int32, (LANES, KEYS), 0)
    return jnp.where(lane == target + w1, 1.0, 0.0).astype(BF)


def expand_kernel(eb, target, rq, rk, out0, out1, spread, out_a, out_b):
    spread[...] = jnp.zeros_like(spread)
    for z1 in range(2):
        for h1 in range(6):
            g = z1 * 6 + h1
            for z2 in range(2):
                off = ((z1 * 2 + z2) * 6 + h1) * GROUP
                for aw in range(2):
                    spread[g * 16 + aw * 6 : g * 16 + aw * 6 + 6, z2 * GROUP : (z2 + 1) * GROUP] = eb[
                        0, aw, :, off : off + GROUP
                    ]
    full = spread[...]
    high = full.astype(BF)
    rest = full - high.astype(F32)
    mid = rest.astype(BF)
    low = (rest - mid.astype(F32)).astype(BF)
    row = lax.broadcasted_iota(jnp.int32, (12, 1), 0)
    tgt = target[...]
    for w1 in range(WW):
        hot = onehot_rows(tgt, w1)
        block = dot(high, hot) + (dot(mid, hot) + dot(low, hot))
        for g in range(12):
            q = g * 12 + w1
            part = block[g * 16 : g * 16 + 12]
            ok0 = rq[0, q : q + 1, :] == rk[0]
            ok1 = rq[1, q : q + 1, :] == rk[1]
            ok = ((row < 6) & ok0) | ((row >= 6) & ok1)
            part = jnp.where(ok, part, NEG_FILL)
            out_a[pl.ds(q, 12, stride=WIN), :] = part[:, 0:128]
            out_b[pl.ds(q, 12, stride=WIN), :] = part[:, 128:256]
    for aw, out in enumerate((out0, out1)):
        heads = []
        for h in range(HEADS):
            rows = slice((aw * HEADS + h) * WIN, (aw * HEADS + h + 1) * WIN)
            heads.append(jnp.concatenate([out_a[rows, :], out_b[rows, 0:16]], axis=1).T)
        heads.append(jnp.zeros((WIN, SPREAD - HEADS * WIN), F32))
        out[...] = jnp.concatenate(heads, axis=1)


def expand(earth_bias, target, rq, rk):
    return pl.pallas_call(
        expand_kernel,
        name="expand_bias",
        out_shape=(shape((WIN, SPREAD), F32),) * 2,
        in_specs=[VMEM] * 4,
        out_specs=(VMEM,) * 2,
        scratch_shapes=[
            pltpu.VMEM((192, LANES), F32),
            pltpu.VMEM((12 * WIN, 128), F32),
            pltpu.VMEM((12 * WIN, 128), F32),
        ],
        compiler_params=params(16),
        cost_estimate=cost(4 * 10**9, 4 * 1024 * 1024),
    )(earth_bias, target, rq, rk)


def windows_kernel(aws, second, *refs):
    refs = list(refs)
    take = lambda n: [refs.pop(0) for _ in range(n)]
    f, u, wq, wk, wv, wo = take(6)
    biases = dict(zip(aws, take(len(aws))))
    near = take(1) if 0 in aws else [None]
    halos = near + (take(3) if 1 in aws else [])
    if second:
        (lon,) = take(1)
    started = second or 1 in aws
    if started:
        (w_in,) = take(1)
    if second:
        gb_in = take(len(aws))
    grads, w_s = take(2)
    gbs = dict(zip(aws, take(len(aws))))
    if second:
        (lon_back,) = take(1)
    x_s, u_s, i_s, low_s, q_s, k_s, v_s, ga_s, gq_s = take(9)
    if second:
        g_s, lon_s = take(2)
    w_s[...] = w_in[...] if started else jnp.zeros_like(w_s)
    for n, aw in enumerate(aws):
        gbs[aw][...] = gb_in[n][...] if second else jnp.zeros_like(gbs[aw])

    for n, aw in enumerate(aws):
        for b in range(2):
            if second:
                halo = split(lon[b * WIN : (b + 1) * WIN, :].astype(F32))
            for z in range(2):
                for h in range(6):
                    lines = source_lines((f, u), halos, aw, b, z, h)
                    row = (n * 2 + b) * WIN + z * 72 + h * 12
                    hrow = (z * 12 + aw * 6 + h) * 6
                    for t, dst in enumerate((x_s, u_s)):
                        if second:
                            dst[row : row + 6, :] = lines[t][18:24]
                            dst[row + 6 : row + 12, :] = halo[t][hrow : hrow + 6]
                        else:
                            dst[row : row + 12, :] = lines[t][6:18]

    raw = x_s[...]
    centred = raw - jnp.mean(raw, axis=-1, keepdims=True)
    inv_std = lax.rsqrt(jnp.mean(centred * centred, axis=-1, keepdims=True) + EPS)
    normed = centred * inv_std
    low = normed.astype(BF)
    x_s[...] = normed
    i_s[...] = inv_std
    low_s[...] = low
    q_s[...] = dot(low, wq[...]).astype(BF)
    k_s[...] = dot(low, wk[...]).astype(BF)
    v_s[...] = dot(low, wv[...]).astype(BF)
    ga_s[...] = dot(u_s[...].astype(BF), wo[...], 1, 1).astype(BF)

    lane = lax.broadcasted_iota(jnp.int32, (1, C), 1)
    picks = [
        jnp.where((lane >= h * HD) & (lane < (h + 1) * HD), 1.0, 0.0).astype(BF)
        for h in range(HEADS)
    ]

    def stack(a):
        pad = jnp.zeros((SPREAD - HEADS * WIN, C), BF)
        return jnp.concatenate([a * m for m in picks] + [pad], axis=0)

    def unstack(a):
        return jnp.concatenate(
            [a[h * HD : (h + 1) * HD, h * WIN : (h + 1) * WIN] for h in range(HEADS)], axis=0
        )

    for w in range(2 * len(aws)):
        rows = slice(w * WIN, (w + 1) * WIN)
        bias, gb_s = biases[aws[w // 2]], gbs[aws[w // 2]]
        low, q, k, v, ga = low_s[rows, :], q_s[rows, :], k_s[rows, :], v_s[rows, :], ga_s[rows, :]
        up = u_s[rows, :].astype(BF)
        qs = stack(q)
        gas = stack(ga)
        scores = dot(k, qs, 1, 1)
        grad_probs = dot(v, gas, 1, 1)
        probs, grads_low = [], []
        for i in range(SPREAD // 128):
            cols = slice(i * 128, (i + 1) * 128)
            s = scores[:, cols] * SCALE + bias[:, cols]
            e = jnp.exp(s - jnp.max(s, axis=0, keepdims=True))
            p = e * (1.0 / jnp.sum(e, axis=0, keepdims=True))
            gp = grad_probs[:, cols]
            gs = p * (gp - jnp.sum(p * gp, axis=0, keepdims=True))
            gb_s[:, cols] += gs
            probs.append(p.astype(BF))
            grads_low.append(gs.astype(BF))
        p = jnp.concatenate(probs, axis=1)
        gs = jnp.concatenate(grads_low, axis=1)
        gv = dot(p, gas).astype(BF)
        gk = (dot(gs, qs) * SCALE).astype(BF)
        att_t = unstack(dot(v, p, 0, 0)).astype(BF)
        gq_t = (unstack(dot(k, gs, 0, 0)) * SCALE).astype(BF)
        w_s[0:C, :] += dot(gq_t, low)
        w_s[C : 2 * C, :] += dot(low, gk, 0, 0)
        w_s[2 * C : 3 * C, :] += dot(low, gv, 0, 0)
        w_s[3 * C : 4 * C, :] += dot(att_t, up)
        gq_s[rows, :] = (
            dot(gq_t, wq[...], 0, 1) + dot(gk, wk[...], 1, 1) + dot(gv, wv[...], 1, 1)
        )

    gu = gq_s[...]
    normed = x_s[...]
    centre = jnp.mean(gu, axis=-1, keepdims=True)
    along = jnp.mean(gu * normed, axis=-1, keepdims=True)
    grad = i_s[...] * (gu - centre - normed * along)
    grads[...] = grad.astype(BF)
    if not second:
        return

    g_s[...] = grad
    for b in range(2):
        for z in range(2):
            for r in range(12):
                row = ((r // 6) * 2 + b) * WIN + z * 72 + (r % 6) * 12
                to = b * WIN + (z * 12 + r) * 6
                lon_s[to : to + 6, :] = g_s[row + 6 : row + 12, :]
    lon_back[...] = lon_s[...].astype(BF)


def fold_kernel(w, gb0, gb1, target, core, keep, send, w_s, turned, slab):
    w_s[C:, :] = w[C:, :]
    w_s[0:C, :] = w[0:C, :].T
    slab[0:768, :] = w_s[:, 0:128].astype(BF)
    slab[768:1152, :] = jnp.concatenate([w_s[0:384, 128:192], w_s[384:768, 128:192]], axis=1).astype(BF)
    for z2 in range(2):
        for aw, gb in enumerate((gb0, gb1)):
            for h in range(HEADS):
                at = ((z2 * 2 + aw) * HEADS + h) * WIN
                rows = slice(z2 * 72, z2 * 72 + 72)
                turned[at : at + WIN, 0:72] = gb[rows, h * WIN : (h + 1) * WIN].T
    folded = jnp.zeros((288, KEYS), F32)
    tgt = target[...]
    lane = lax.broadcasted_iota(jnp.int32, (KEYS, 72), 0)
    for w1 in range(WW):
        rows = [turned[pl.ds(g * 12 + w1, 24, stride=WIN), :] for g in range(12)]
        full = jnp.concatenate(rows, axis=0)[:, 0:72].astype(BF)
        hot = jnp.where(lane == tgt[:, 0:72] + w1, 1.0, 0.0).astype(BF)
        folded = folded + dot(full, hot, 1, 1)
    slab[1152:1440, :] = folded[:, 0:128].astype(BF)
    rest = [folded[24 * i : 24 * i + 24, 128:138] for i in range(12)]
    rest = jnp.concatenate(rest + [jnp.zeros((24, 8), F32)], axis=1)
    slab[1440:1536, :] = jnp.concatenate([rest, jnp.zeros((72, 128), F32)], axis=0).astype(BF)
    top = pl.multiple_of(core[0, 0] * SIDE, SIDE)
    keep[...] = slab[pl.ds(top, SIDE), :]
    send[...] = slab[pl.ds(SIDE - top, SIDE), :]


def fold(w, gb0, gb1, target, core):
    return pl.pallas_call(
        fold_kernel,
        name="fold",
        out_shape=(shape((SIDE, 128), BF),) * 2,
        in_specs=[VMEM] * 4 + [SMEM],
        out_specs=(VMEM,) * 2,
        scratch_shapes=[
            pltpu.VMEM((4 * C, C), F32),
            pltpu.VMEM((24 * WIN, 128), F32),
            pltpu.VMEM((SLAB, 128), BF),
        ],
        compiler_params=params(24),
        cost_estimate=cost(2 * 10**9, 4 * 1024 * 1024),
    )(w, gb0, gb1, target, core)


def windows(aws, second, *args):
    tokens = len(aws) * PAIR
    rows = [pltpu.VMEM((tokens, C), F32)] * 2 + [pltpu.VMEM((tokens, 1), F32)]
    rows += [pltpu.VMEM((tokens, C), BF)] * 5 + [pltpu.VMEM((tokens, C), F32)]
    outs = (shape((tokens, C), BF), shape((4 * C, C), F32))
    outs += (shape((WIN, SPREAD), F32),) * len(aws)
    if second:
        outs += (shape((2 * WIN, C), BF),)
        rows += [pltpu.VMEM((tokens, C), F32), pltpu.VMEM((2 * WIN, C), F32)]
    return pl.pallas_call(
        functools.partial(windows_kernel, aws, second),
        name="windows_second" if second else "windows_upper" if 1 in aws else "windows_lower",
        out_shape=outs,
        in_specs=[VMEM] * len(args),
        out_specs=(VMEM,) * len(outs),
        scratch_shapes=rows,
        compiler_params=params(28),
        cost_estimate=cost(3 * 10**9 * len(aws), 4 * 1024 * 1024),
    )(*args)


def merge_kernel(g_lower, g_upper, g_second, lon_in, own, lev, lat, diag):
    for b in range(2):
        halo = lon_in[b * WIN : (b + 1) * WIN, :].astype(F32)
        for aw, g_first in enumerate((g_lower, g_upper)):
            first = g_first[b * WIN : (b + 1) * WIN, :].astype(F32)
            second = g_second[(aw * 2 + b) * WIN : (aw * 2 + b + 1) * WIN, :].astype(F32)
            for z in range(2):
                for h in range(6):
                    r = aw * 6 + h
                    off = z * 72 + h * 12
                    hrow = (z * 12 + r) * 6
                    line = jnp.concatenate(
                        [halo[hrow : hrow + 6], first[off : off + 12], second[off : off + 6]], axis=0
                    ).astype(BF)
                    if z == 0:
                        if r < 9:
                            own[b, r] = line
                        else:
                            lat[b, r - 9] = line
                    elif r < 9:
                        lev[b, r] = line
                    else:
                        diag[b, r - 9] = line


def merge(*args):
    return pl.pallas_call(
        merge_kernel,
        name="merge_lon",
        out_shape=(
            shape((2, 9, 24, C), BF),
            shape((2, 9, 24, C), BF),
            shape((2, 3, 24, C), BF),
            shape((2, 3, 24, C), BF),
        ),
        in_specs=[VMEM] * 4,
        out_specs=(VMEM,) * 4,
        compiler_params=params(16),
        cost_estimate=cost(2 * 10**10, 2 * 1024 * 1024),
    )(*args)


def place_kernel(own, lev, lat, diag, out):
    for b in range(2):
        out[b, 1, 3:12] = own[b].astype(F32)
        out[b, 1, 0:3] = lat[b].astype(F32)
        out[b, 0, 3:12] = lev[b].astype(F32)
        out[b, 0, 0:3] = diag[b].astype(F32)


def place(own, lev, lat, diag):
    return pl.pallas_call(
        place_kernel,
        name="place_grad",
        out_shape=shape((2, 2, 12, 24, C), F32),
        in_specs=[VMEM] * 4,
        out_specs=VMEM,
        compiler_params=params(16),
        cost_estimate=cost(2 * 10**10, 2 * 1024 * 1024),
    )(own, lev, lat, diag)


def finish_kernel(factor, half, other, core, qkv, out, bias, slab):
    top = pl.multiple_of(core[0, 0] * SIDE, SIDE)
    slab[pl.ds(top, SIDE), :] = half[...].astype(F32)
    slab[pl.ds(SIDE - top, SIDE), :] = other[...].astype(F32)
    full = slab[...]
    right = full[768:1152]
    rest = jnp.concatenate([right[:, 0:64], right[:, 64:128]], axis=0)
    whole = jnp.concatenate([full[0:768], rest], axis=1) * factor
    for j in range(3):
        qkv[:, j * C : (j + 1) * C] = whole[j * C : (j + 1) * C]
    out[...] = whole[3 * C : 4 * C]
    tail = full[1440:1464]
    tail = jnp.concatenate([tail[:, 10 * i : 10 * i + 10] for i in range(12)], axis=0)
    pairs = jnp.concatenate([full[1152:1440], tail], axis=1)
    for z1 in range(2):
        for h1 in range(6):
            for z2 in range(2):
                off = ((z1 * 2 + z2) * 6 + h1) * GROUP
                for aw in range(2):
                    at = (z1 * 6 + h1) * 24 + z2 * 12 + aw * 6
                    bias[0, aw, :, off : off + GROUP] = pairs[at : at + 6]


def finish(half, other, core, factor):
    return pl.pallas_call(
        functools.partial(finish_kernel, factor),
        name="finish_params",
        out_shape=(
            shape((C, 3 * C), F32),
            shape((C, C), F32),
            shape((1, 2, HEADS, PAIRS), F32),
        ),
        in_specs=[VMEM, VMEM, SMEM],
        out_specs=(VMEM,) * 3,
        scratch_shapes=[pltpu.VMEM((SLAB, 128), F32)],
        compiler_params=params(16),
        cost_estimate=cost(0, 2 * 1024 * 1024),
    )(half, other, core)


def from_behind(x, axis, by):
    devices = lax.axis_size(axis)
    return lax.ppermute(x, axis, [(i, (i + by) % devices) for i in range(devices)])


def from_corner(x, by):
    lats, levs = lax.axis_size("lat"), lax.axis_size("lev")
    pairs = [
        (a * levs + v, ((a + by) % lats) * levs + (v + by) % levs)
        for a in range(lats)
        for v in range(levs)
    ]
    return lax.ppermute(x, ("lat", "lev"), pairs)


def other_core(x):
    return lax.ppermute(x, "lon", [(i, i ^ 1) for i in range(lax.axis_size("lon"))])


def reduce_slab(keep, send):
    lons, lats, levs = (lax.axis_size(a) for a in ("lon", "lat", "lev"))
    depth = lons // 4
    rows = SIDE // depth
    along = [[4 * z + low for z in range(depth)] for low in range(4)]
    plane = [
        [((4 * z + 2 * y + c) * lats + a) * levs + v for y in range(2) for a in range(lats) for v in range(levs)]
        for z in range(depth)
        for c in range(2)
    ]
    half = (keep.astype(F32) + other_core(send).astype(F32)).astype(BF)
    pieces = lax.all_to_all(
        half.reshape(depth, rows, 128), "lon", 0, 0, axis_index_groups=along, tiled=True
    )
    mine = jnp.sum(pieces.astype(F32), axis=0).astype(BF)
    count = 2 * lats * levs
    every = lax.all_to_all(
        jnp.broadcast_to(mine[None], (count, rows, 128)),
        ("lon", "lat", "lev"), 0, 0, axis_index_groups=plane, tiled=True,
    )
    lon = lax.axis_index("lon")
    first = (lon % 2) * SIDE + (lon // 4) * rows
    spot = jnp.arange(count, dtype=jnp.int32) % (lats * levs)
    same = spot == lax.axis_index("lat") * levs + lax.axis_index("lev")
    picked = jnp.where(same | (first < WROWS), 1.0, 0.0).astype(F32)
    mine = jnp.sum(every.astype(F32) * picked[:, None, None], axis=0).astype(BF)
    half = lax.all_to_all(
        jnp.broadcast_to(mine[None], (depth, rows, 128)), "lon", 0, 0, axis_index_groups=along, tiled=True
    ).reshape(SIDE, 128)
    return half, other_core(half)


def body(fields, upstream, qkv_weight, out_weight, earth_bias):
    near = from_behind(pack_near(fields, upstream), "lev", -1)
    far_msg, lat_msg, diag_msg = pack_rest(fields, upstream)
    far = from_behind(far_msg, "lev", -1)
    lat = from_behind(lat_msg, "lat", -1)
    diag = from_corner(diag_msg, -1)

    key = jnp.arange(WIN, dtype=jnp.int32)
    target = (key // WW) * OFFS - key % WW + WW - 1
    target = jnp.concatenate([target, jnp.full((KEYS - WIN,), -1000, jnp.int32)])[None, :]
    last_lev = lax.axis_index("lev") == lax.axis_size("lev") - 1
    last_lat = lax.axis_index("lat") == lax.axis_size("lat") - 1
    lev_flag = ((key // 72) == 1) & last_lev
    lat_flag = ((key // WW) % WH >= WH // 2) & last_lat
    region = jnp.stack(
        [2 * lev_flag.astype(F32), 2 * lev_flag.astype(F32) + lat_flag.astype(F32)]
    )
    keys = jnp.concatenate([region, jnp.zeros((2, KEYS - WIN), F32)], axis=1)
    bias0, bias1 = expand(earth_bias, target, region[:, :, None], keys[:, None, :])
    core = (lax.axis_index("lon") % 2).astype(jnp.int32).reshape(1, 1)

    shared = (
        fields, upstream,
        qkv_weight[:, 0:C], qkv_weight[:, C : 2 * C], qkv_weight[:, 2 * C :], out_weight,
    )
    g_lower, w, gb0 = windows((0,), False, *shared, bias0, near)
    rest = (far, lat, diag)
    lon = from_behind(pack_lon(fields, upstream, (near,) + rest), "lon", -1)
    g_upper, w, gb1 = windows((1,), False, *shared, bias1, *rest, w)
    g_second, w, gb0, gb1, lon_back = windows(
        (0, 1), True, *shared, bias0, bias1, near, *rest, lon, w, gb0, gb1
    )
    keep, send = fold(w, gb0, gb1, target, core)
    half, other = reduce_slab(keep, send)
    lon_in = from_behind(lon_back, "lon", 1)
    own, lev_out, lat_out, diag_out = merge(g_lower, g_upper, g_second, lon_in)
    lev_in = from_behind(lev_out, "lev", 1)
    lat_in = from_behind(lat_out, "lat", 1)
    diag_in = from_corner(diag_out, 1)
    field_grad = place(own, lev_in, lat_in, diag_in)

    samples, levels, rows, cols, _ = fields.shape
    tokens = samples * levels * rows * cols
    for axis in ("lon", "lat", "lev"):
        tokens = tokens * lax.axis_size(axis)
    qkv_grad, out_grad, bias_grad = finish(half, other, core, 1.0 / math.sqrt(tokens))
    return (field_grad, qkv_grad, out_grad, bias_grad)


def solution(mesh):
    return jax.shard_map(
        body,
        mesh=mesh,
        in_specs=(
            P(None, "lev", "lat", "lon", None),
            P(None, "lev", "lat", "lon", None),
            P(),
            P(),
            P("lev", "lat", None, None),
        ),
        out_specs=(P(None, "lev", "lat", "lon", None), P(), P(), P("lev", "lat", None, None)),
        check_vma=False,
    )
```

```python
import functools
import math

import jax
import jax.numpy as jnp
from jax import lax
from jax.experimental import pallas as pl
from jax.experimental.pallas import tpu as pltpu
from jax.sharding import PartitionSpec as P

HEADS = 6
WZ = 2
WH = 6
WW = 12
WIN = 144
PAIRS = 3312
C = 192
HD = 32
OFFS = 2 * WW - 1
GROUP = WH * OFFS
LANES = 384
KEYS = 256
NEG_FILL = -1e30
EPS = 1e-05
SCALE = HD**-0.5
SLAB = 1536
SIDE = SLAB // 2
WROWS = 1152
BF = jnp.bfloat16
F32 = jnp.float32
SPREAD = 896
MAIN = 128
TAIL = WIN - MAIN
TAILS = HEADS * MAIN
PAIR = 2 * WIN
BOTH = 2 * C
VMEM = pl.BlockSpec(memory_space=pltpu.VMEM)
HBM = pl.BlockSpec(memory_space=pl.ANY)
SMEM = pl.BlockSpec(memory_space=pltpu.SMEM)


def params(mib):
    return pltpu.CompilerParams(vmem_limit_bytes=mib * 1024 * 1024)


def cost(flops, nbytes):
    return pl.CostEstimate(flops=flops, bytes_accessed=nbytes, transcendentals=0)


def dot(a, b, ca=1, cb=0):
    return lax.dot_general(a, b, (((ca,), (cb,)), ((), ())), preferred_element_type=F32)


def shape(dims, dtype):
    return jax.ShapeDtypeStruct(dims, dtype)


def join(a, b):
    return jnp.concatenate([a[:, 0:128], b[:, 0:128], a[:, 128:C], b[:, 128:C]], axis=1)


def split(m):
    return (
        jnp.concatenate([m[:, 0:128], m[:, 256:320]], axis=1),
        jnp.concatenate([m[:, 128:256], m[:, 320:384]], axis=1),
    )


def pack_near_kernel(f, u, near):
    for b in range(2):
        for h in range(6):
            near[b, h] = join(f[b, 0, h + 3], u[b, 0, h + 3])


def pack_near(fields, upstream):
    return pl.pallas_call(
        pack_near_kernel,
        name="pack_near",
        out_shape=shape((2, 6, 24, BOTH), BF),
        in_specs=[VMEM] * 2,
        out_specs=VMEM,
        compiler_params=params(16),
        cost_estimate=cost(0, 2 * 1024 * 1024),
    )(fields, upstream)


def pack_rest_kernel(f, u, far, lat, diag):
    for b in range(2):
        for r in range(3):
            far[b, r] = join(f[b, 0, r + 9], u[b, 0, r + 9])
            lat[b, r] = join(f[b, 1, r], u[b, 1, r])
            diag[b, r] = join(f[b, 0, r], u[b, 0, r])


def pack_rest(fields, upstream):
    return pl.pallas_call(
        pack_rest_kernel,
        name="pack_rest",
        out_shape=(shape((2, 3, 24, BOTH), BF),) * 3,
        in_specs=[VMEM] * 2,
        out_specs=(VMEM,) * 3,
        compiler_params=params(16),
        cost_estimate=cost(0, 2 * 1024 * 1024),
    )(fields, upstream)


def source_lines(own, halos, aw, b, z, h):
    if z == 0 and (aw == 0 or h < 3):
        return [a[b, 1, 6 * aw + h + 3].astype(F32) for a in own]
    if aw == 0:
        line = halos[0][b, h]
    elif z == 0:
        line = halos[2][b, h - 3]
    else:
        line = halos[1][b, h] if h < 3 else halos[3][b, h - 3]
    return split(line.astype(F32))


def pack_lon_kernel(f, u, near, far, lat, diag, after, out, tmp):
    for b in range(2):
        for z in range(2):
            for r in range(12):
                lines = source_lines((f, u), (near, far, lat, diag), r // 6, b, z, r % 6)
                row = b * WIN + (z * 12 + r) * 6
                tmp[row : row + 6, :] = join(lines[0][0:6], lines[1][0:6])
    out[...] = tmp[...].astype(BF)


def pack_lon(fields, upstream, halos, after):
    return pl.pallas_call(
        pack_lon_kernel,
        name="pack_lon",
        out_shape=shape((2 * WIN, BOTH), BF),
        in_specs=[VMEM] * 6 + [HBM],
        out_specs=VMEM,
        scratch_shapes=[pltpu.VMEM((2 * WIN, BOTH), F32)],
        compiler_params=params(16),
        cost_estimate=cost(0, 2 * 1024 * 1024),
    )(fields, upstream, *halos, after)


def onehot_rows(target, w1):
    lane = lax.broadcasted_iota(jnp.int32, (LANES, KEYS), 0)
    return jnp.where(lane == target + w1, 1.0, 0.0).astype(BF)


def expand_kernel(eb, target, rq, rk, out0, out1, spread, out_a, out_b):
    spread[...] = jnp.zeros_like(spread)
    for z1 in range(2):
        for h1 in range(6):
            g = z1 * 6 + h1
            for z2 in range(2):
                off = ((z1 * 2 + z2) * 6 + h1) * GROUP
                for aw in range(2):
                    spread[g * 16 + aw * 6 : g * 16 + aw * 6 + 6, z2 * GROUP : (z2 + 1) * GROUP] = eb[
                        0, aw, :, off : off + GROUP
                    ]
    full = spread[...]
    high = full.astype(BF)
    rest = full - high.astype(F32)
    mid = rest.astype(BF)
    low = (rest - mid.astype(F32)).astype(BF)
    row = lax.broadcasted_iota(jnp.int32, (12, 1), 0)
    tgt = target[...]
    for w1 in range(WW):
        hot = onehot_rows(tgt, w1)
        block = dot(high, hot) + (dot(mid, hot) + dot(low, hot))
        for g in range(12):
            q = g * 12 + w1
            part = block[g * 16 : g * 16 + 12]
            ok0 = rq[0, q : q + 1, :] == rk[0]
            ok1 = rq[1, q : q + 1, :] == rk[1]
            ok = ((row < 6) & ok0) | ((row >= 6) & ok1)
            part = jnp.where(ok, part, NEG_FILL)
            out_a[pl.ds(q, 12, stride=WIN), :] = part[:, 0:128]
            out_b[pl.ds(q, 12, stride=WIN), :] = part[:, 128:256]
    for aw, out in enumerate((out0, out1)):
        tails = []
        for h in range(HEADS):
            rows = slice((aw * HEADS + h) * WIN, (aw * HEADS + h + 1) * WIN)
            turned = jnp.concatenate([out_a[rows, :], out_b[rows, 0:16]], axis=1).T
            out[:, h * MAIN : (h + 1) * MAIN] = turned[:, 0:MAIN]
            tails.append(turned[:, MAIN:WIN])
        tails.append(jnp.zeros((WIN, SPREAD - HEADS * WIN), F32))
        out[:, TAILS:SPREAD] = jnp.concatenate(tails, axis=1)


def expand(earth_bias, target, rq, rk):
    return pl.pallas_call(
        expand_kernel,
        name="expand_bias",
        out_shape=(shape((WIN, SPREAD), F32),) * 2,
        in_specs=[VMEM] * 4,
        out_specs=(VMEM,) * 2,
        scratch_shapes=[
            pltpu.VMEM((192, LANES), F32),
            pltpu.VMEM((12 * WIN, 128), F32),
            pltpu.VMEM((12 * WIN, 128), F32),
        ],
        compiler_params=params(16),
        cost_estimate=cost(4 * 10**9, 4 * 1024 * 1024),
    )(earth_bias, target, rq, rk)


def windows_kernel(aws, second, *refs):
    refs = list(refs)
    take = lambda n: [refs.pop(0) for _ in range(n)]
    f, u, wq, wk, wv, wo = take(6)
    biases = dict(zip(aws, take(len(aws))))
    near = take(1) if 0 in aws else [None]
    halos = near + (take(3) if 1 in aws else [])
    if second:
        (lon,) = take(1)
    started = second or 1 in aws
    if started:
        (w_in,) = take(1)
    if second:
        gb_in = take(len(aws))
    grads, w_s = take(2)
    gbs = dict(zip(aws, take(len(aws))))
    if second:
        (lon_back,) = take(1)
    x_s, u_s, i_s, low_s, q_s, k_s, v_s, ga_s, gq_s, gk_s, gv_s, att_s, up_s = take(13)
    if second:
        g_s, lon_s = take(2)
    w_s[...] = w_in[...] if started else jnp.zeros_like(w_s)
    for n, aw in enumerate(aws):
        gbs[aw][...] = gb_in[n][...] if second else jnp.zeros_like(gbs[aw])

    for n, aw in enumerate(aws):
        for b in range(2):
            if second:
                halo = split(lon[b * WIN : (b + 1) * WIN, :].astype(F32))
            for z in range(2):
                for h in range(6):
                    lines = source_lines((f, u), halos, aw, b, z, h)
                    row = (n * 2 + b) * WIN + z * 72 + h * 12
                    hrow = (z * 12 + aw * 6 + h) * 6
                    for t, dst in enumerate((x_s, u_s)):
                        if second:
                            dst[row : row + 6, :] = lines[t][18:24]
                            dst[row + 6 : row + 12, :] = halo[t][hrow : hrow + 6]
                        else:
                            dst[row : row + 12, :] = lines[t][6:18]

    raw = x_s[...]
    centred = raw - jnp.mean(raw, axis=-1, keepdims=True)
    inv_std = lax.rsqrt(jnp.mean(centred * centred, axis=-1, keepdims=True) + EPS)
    normed = centred * inv_std
    low = normed.astype(BF)
    x_s[...] = normed
    i_s[...] = inv_std
    low_s[...] = low
    q_s[...] = dot(low, wq[...]).astype(BF)
    k_s[...] = dot(low, wk[...]).astype(BF)
    v_s[...] = dot(low, wv[...]).astype(BF)
    up = u_s[...].astype(BF)
    ga_s[...] = dot(up, wo[...], 1, 1).astype(BF)
    att_s[...] = jnp.zeros_like(att_s)
    up_s[...] = jnp.zeros_like(up_s)
    for w in range(2 * len(aws)):
        up_s[w * KEYS : w * KEYS + WIN, :] = up[w * WIN : (w + 1) * WIN]

    lane = lax.broadcasted_iota(jnp.int32, (1, C), 1)
    picks = [
        jnp.where((lane >= h * HD) & (lane < (h + 1) * HD), 1.0, 0.0).astype(BF)
        for h in range(HEADS)
    ]

    def stack(a):
        pad = jnp.zeros((SPREAD - HEADS * WIN, C), BF)
        mains = [a[0:MAIN] * m for m in picks]
        return jnp.concatenate(mains + [a[MAIN:WIN] * m for m in picks] + [pad], axis=0)

    def per_head(a, probs):
        tails = dot(a, probs[:, TAILS:SPREAD])
        heads = []
        for i in range(HEADS // 2):
            pair = dot(a[2 * i * HD : 2 * (i + 1) * HD], probs[:, 2 * i * MAIN : 2 * (i + 1) * MAIN])
            for n in range(2):
                h = 2 * i + n
                main = pair[n * HD : (n + 1) * HD, n * MAIN : (n + 1) * MAIN]
                tail = tails[h * HD : (h + 1) * HD, h * TAIL : (h + 1) * TAIL]
                heads.append(jnp.concatenate([main, tail], axis=1))
        return jnp.concatenate(heads, axis=0)

    for w in range(2 * len(aws)):
        rows = slice(w * WIN, (w + 1) * WIN)
        bias, gb_s = biases[aws[w // 2]], gbs[aws[w // 2]]
        low, q, k, v, ga = low_s[rows, :], q_s[rows, :], k_s[rows, :], v_s[rows, :], ga_s[rows, :]
        qs = stack(q)
        gas = stack(ga)
        scores = dot(k, qs, 1, 1)
        grad_probs = dot(v, gas, 1, 1)
        probs, grads_low = [], []
        for i in range(SPREAD // 128):
            cols = slice(i * 128, (i + 1) * 128)
            s = scores[:, cols] * SCALE + bias[:, cols]
            e = jnp.exp(s - jnp.max(s, axis=0, keepdims=True))
            p = e * (1.0 / jnp.sum(e, axis=0, keepdims=True))
            gp = grad_probs[:, cols]
            gs = p * (gp - jnp.sum(p * gp, axis=0, keepdims=True))
            gb_s[:, cols] += gs
            probs.append(p.astype(BF))
            grads_low.append(gs.astype(BF))
        p = jnp.concatenate(probs, axis=1)
        gs = jnp.concatenate(grads_low, axis=1)
        gv_s[rows, :] = dot(p, gas).astype(BF)
        gk_s[rows, :] = (dot(gs, qs) * SCALE).astype(BF)
        gq_s[rows, :] = (per_head(k.T, gs) * SCALE).T.astype(BF)
        att_s[:, w * KEYS : w * KEYS + WIN] = per_head(v.T, p).astype(BF)

    w_s[3 * C : 4 * C, :] += dot(att_s[...], up_s[...])
    gq, gk, gv = gq_s[...], gk_s[...], gv_s[...]
    low_t = low_s[...].T
    w_s[0:C, :] += dot(low_t, gq)
    w_s[C : 2 * C, :] += dot(low_t, gk)
    w_s[2 * C : 3 * C, :] += dot(low_t, gv)
    gu = dot(gq, wq[...], 1, 1) + dot(gk, wk[...], 1, 1) + dot(gv, wv[...], 1, 1)
    normed = x_s[...]
    centre = jnp.mean(gu, axis=-1, keepdims=True)
    along = jnp.mean(gu * normed, axis=-1, keepdims=True)
    grad = i_s[...] * (gu - centre - normed * along)
    grads[...] = grad.astype(BF)
    if not second:
        return

    g_s[...] = grad
    for b in range(2):
        for z in range(2):
            for r in range(12):
                row = ((r // 6) * 2 + b) * WIN + z * 72 + (r % 6) * 12
                to = b * WIN + (z * 12 + r) * 6
                lon_s[to : to + 6, :] = g_s[row + 6 : row + 12, :]
    lon_back[...] = lon_s[...].astype(BF)


def fold_kernel(w_s, gb0, gb1, target, core, keep, send, turned, slab):
    slab[0:768, :] = w_s[:, 0:128].astype(BF)
    slab[768:1152, :] = jnp.concatenate([w_s[0:384, 128:192], w_s[384:768, 128:192]], axis=1).astype(BF)
    for z2 in range(2):
        for aw, gb in enumerate((gb0, gb1)):
            rows = slice(z2 * 72, z2 * 72 + 72)
            tails = gb[rows, TAILS:SPREAD].T
            for h in range(HEADS):
                at = ((z2 * HEADS + h) * 2 + aw) * WIN
                turned[at : at + MAIN, 0:72] = gb[rows, h * MAIN : (h + 1) * MAIN].T
                turned[at + MAIN : at + WIN, 0:72] = tails[h * TAIL : (h + 1) * TAIL]
    folded = jnp.zeros((288, KEYS), F32)
    tgt = target[...]
    lane = lax.broadcasted_iota(jnp.int32, (KEYS, 72), 0)
    for w1 in range(WW):
        rows = [turned[pl.ds(g * 12 + w1, 24, stride=WIN), :] for g in range(12)]
        full = jnp.concatenate(rows, axis=0)[:, 0:72].astype(BF)
        hot = jnp.where(lane == tgt[:, 0:72] + w1, 1.0, 0.0).astype(BF)
        folded = folded + dot(full, hot, 1, 1)
    slab[1152:1440, :] = folded[:, 0:128].astype(BF)
    rest = [folded[24 * i : 24 * i + 24, 128:138] for i in range(12)]
    rest = jnp.concatenate(rest + [jnp.zeros((24, 8), F32)], axis=1)
    slab[1440:1536, :] = jnp.concatenate([rest, jnp.zeros((72, 128), F32)], axis=0).astype(BF)
    top = pl.multiple_of(core[0, 0] * SIDE, SIDE)
    keep[...] = slab[pl.ds(top, SIDE), :]
    send[...] = slab[pl.ds(SIDE - top, SIDE), :]


def fold(w, gb0, gb1, target, core):
    return pl.pallas_call(
        fold_kernel,
        name="fold",
        out_shape=(shape((SIDE, 128), BF),) * 2,
        in_specs=[VMEM] * 4 + [SMEM],
        out_specs=(VMEM,) * 2,
        scratch_shapes=[
            pltpu.VMEM((24 * WIN, 128), F32),
            pltpu.VMEM((SLAB, 128), BF),
        ],
        compiler_params=params(24),
        cost_estimate=cost(2 * 10**9, 4 * 1024 * 1024),
    )(w, gb0, gb1, target, core)


def windows(aws, second, *args):
    tokens = len(aws) * PAIR
    rows = [pltpu.VMEM((tokens, C), F32)] * 2 + [pltpu.VMEM((tokens, 1), F32)]
    rows += [pltpu.VMEM((tokens, C), BF)] * 8
    padded = 2 * len(aws) * KEYS
    rows += [pltpu.VMEM((C, padded), BF), pltpu.VMEM((padded, C), BF)]
    outs = (shape((tokens, C), BF), shape((4 * C, C), F32))
    outs += (shape((WIN, SPREAD), F32),) * len(aws)
    if second:
        outs += (shape((2 * WIN, C), BF),)
        rows += [pltpu.VMEM((tokens, C), F32), pltpu.VMEM((2 * WIN, C), F32)]
    return pl.pallas_call(
        functools.partial(windows_kernel, aws, second),
        name="windows_second" if second else "windows_upper" if 1 in aws else "windows_lower",
        out_shape=outs,
        in_specs=[VMEM] * len(args),
        out_specs=(VMEM,) * len(outs),
        scratch_shapes=rows,
        compiler_params=params(28),
        cost_estimate=cost(3 * 10**9 * len(aws), 4 * 1024 * 1024),
    )(*args)


def merge_kernel(g_lower, g_upper, g_second, lon_in, own, lev, lat, diag):
    for b in range(2):
        halo = lon_in[b * WIN : (b + 1) * WIN, :].astype(F32)
        for aw, g_first in enumerate((g_lower, g_upper)):
            first = g_first[b * WIN : (b + 1) * WIN, :].astype(F32)
            second = g_second[(aw * 2 + b) * WIN : (aw * 2 + b + 1) * WIN, :].astype(F32)
            for z in range(2):
                for h in range(6):
                    r = aw * 6 + h
                    off = z * 72 + h * 12
                    hrow = (z * 12 + r) * 6
                    line = jnp.concatenate(
                        [halo[hrow : hrow + 6], first[off : off + 12], second[off : off + 6]], axis=0
                    ).astype(BF)
                    if z == 0:
                        if r < 9:
                            own[b, r] = line
                        else:
                            lat[b, r - 9] = line
                    elif r < 9:
                        lev[b, r] = line
                    else:
                        diag[b, r - 9] = line


def merge(*args):
    return pl.pallas_call(
        merge_kernel,
        name="merge_lon",
        out_shape=(
            shape((2, 9, 24, C), BF),
            shape((2, 9, 24, C), BF),
            shape((2, 3, 24, C), BF),
            shape((2, 3, 24, C), BF),
        ),
        in_specs=[VMEM] * 4,
        out_specs=(VMEM,) * 4,
        compiler_params=params(16),
        cost_estimate=cost(2 * 10**10, 2 * 1024 * 1024),
    )(*args)


def place_kernel(own, lev, lat, diag, out):
    for b in range(2):
        out[b, 1, 3:12] = own[b].astype(F32)
        out[b, 1, 0:3] = lat[b].astype(F32)
        out[b, 0, 3:12] = lev[b].astype(F32)
        out[b, 0, 0:3] = diag[b].astype(F32)


def place(own, lev, lat, diag):
    return pl.pallas_call(
        place_kernel,
        name="place_grad",
        out_shape=shape((2, 2, 12, 24, C), F32),
        in_specs=[VMEM] * 4,
        out_specs=VMEM,
        compiler_params=params(16),
        cost_estimate=cost(2 * 10**10, 2 * 1024 * 1024),
    )(own, lev, lat, diag)


def finish_kernel(factor, half, other, core, qkv, out, bias, slab):
    top = pl.multiple_of(core[0, 0] * SIDE, SIDE)
    slab[pl.ds(top, SIDE), :] = half[...].astype(F32)
    slab[pl.ds(SIDE - top, SIDE), :] = other[...].astype(F32)
    full = slab[...]
    right = full[768:1152]
    rest = jnp.concatenate([right[:, 0:64], right[:, 64:128]], axis=0)
    whole = jnp.concatenate([full[0:768], rest], axis=1) * factor
    for j in range(3):
        qkv[:, j * C : (j + 1) * C] = whole[j * C : (j + 1) * C]
    out[...] = whole[3 * C : 4 * C]
    tail = full[1440:1464]
    tail = jnp.concatenate([tail[:, 10 * i : 10 * i + 10] for i in range(12)], axis=0)
    pairs = jnp.concatenate([full[1152:1440], tail], axis=1)
    for z1 in range(2):
        for h1 in range(6):
            for z2 in range(2):
                off = ((z1 * 2 + z2) * 6 + h1) * GROUP
                at = (z1 * 6 + h1) * 24 + z2 * 12
                bias[0, :, :, off : off + GROUP] = pairs[at : at + 12].reshape(HEADS, 2, GROUP)


def finish(half, other, core, factor):
    return pl.pallas_call(
        functools.partial(finish_kernel, factor),
        name="finish_params",
        out_shape=(
            shape((C, 3 * C), F32),
            shape((C, C), F32),
            shape((1, HEADS, 2, PAIRS), F32),
        ),
        in_specs=[VMEM, VMEM, SMEM],
        out_specs=(VMEM,) * 3,
        scratch_shapes=[pltpu.VMEM((SLAB, 128), F32)],
        compiler_params=params(16),
        cost_estimate=cost(0, 2 * 1024 * 1024),
    )(half, other, core)


def from_behind(x, axis, by):
    devices = lax.axis_size(axis)
    return lax.ppermute(x, axis, [(i, (i + by) % devices) for i in range(devices)])


def from_corner(x, by):
    lats, levs = lax.axis_size("lat"), lax.axis_size("lev")
    pairs = [
        (a * levs + v, ((a + by) % lats) * levs + (v + by) % levs)
        for a in range(lats)
        for v in range(levs)
    ]
    return lax.ppermute(x, ("lat", "lev"), pairs)


def other_core(x):
    return lax.ppermute(x, "lon", [(i, i ^ 1) for i in range(lax.axis_size("lon"))])


def reduce_slab(keep, send):
    lons, lats, levs = (lax.axis_size(a) for a in ("lon", "lat", "lev"))
    depth = lons // 4
    rows = SIDE // depth
    along = [[4 * z + low for z in range(depth)] for low in range(4)]
    plane = [
        [((4 * z + 2 * y + c) * lats + a) * levs + v for y in range(2) for a in range(lats) for v in range(levs)]
        for z in range(depth)
        for c in range(2)
    ]
    half = (keep.astype(F32) + other_core(send).astype(F32)).astype(BF)
    pieces = lax.all_to_all(
        half.reshape(depth, rows, 128), "lon", 0, 0, axis_index_groups=along, tiled=True
    )
    mine = jnp.sum(pieces.astype(F32), axis=0).astype(BF)
    count = 2 * lats * levs
    every = lax.all_to_all(
        jnp.broadcast_to(mine[None], (count, rows, 128)),
        ("lon", "lat", "lev"), 0, 0, axis_index_groups=plane, tiled=True,
    )
    lon = lax.axis_index("lon")
    first = (lon % 2) * SIDE + (lon // 4) * rows
    spot = jnp.arange(count, dtype=jnp.int32) % (lats * levs)
    same = spot == lax.axis_index("lat") * levs + lax.axis_index("lev")
    picked = jnp.where(same | (first < WROWS), 1.0, 0.0).astype(F32)
    mine = jnp.sum(every.astype(F32) * picked[:, None, None], axis=0).astype(BF)
    half = lax.all_to_all(
        jnp.broadcast_to(mine[None], (depth, rows, 128)), "lon", 0, 0, axis_index_groups=along, tiled=True
    ).reshape(SIDE, 128)
    return half, other_core(half)


def body(fields, upstream, qkv_weight, out_weight, earth_bias):
    near = from_behind(pack_near(fields, upstream), "lev", -1)
    far_msg, lat_msg, diag_msg = pack_rest(fields, upstream)
    far = from_behind(far_msg, "lev", -1)
    lat = from_behind(lat_msg, "lat", -1)
    diag = from_corner(diag_msg, -1)

    key = jnp.arange(WIN, dtype=jnp.int32)
    target = (key // WW) * OFFS - key % WW + WW - 1
    target = jnp.concatenate([target, jnp.full((KEYS - WIN,), -1000, jnp.int32)])[None, :]
    last_lev = lax.axis_index("lev") == lax.axis_size("lev") - 1
    last_lat = lax.axis_index("lat") == lax.axis_size("lat") - 1
    lev_flag = ((key // 72) == 1) & last_lev
    lat_flag = ((key // WW) % WH >= WH // 2) & last_lat
    region = jnp.stack(
        [2 * lev_flag.astype(F32), 2 * lev_flag.astype(F32) + lat_flag.astype(F32)]
    )
    keys = jnp.concatenate([region, jnp.zeros((2, KEYS - WIN), F32)], axis=1)
    bias0, bias1 = expand(earth_bias, target, region[:, :, None], keys[:, None, :])
    core = (lax.axis_index("lon") % 2).astype(jnp.int32).reshape(1, 1)

    shared = (
        fields, upstream,
        qkv_weight[:, 0:C], qkv_weight[:, C : 2 * C], qkv_weight[:, 2 * C :], out_weight,
    )
    g_lower, w, gb0 = windows((0,), False, *shared, bias0, near)
    rest = (far, lat, diag)
    lon = from_behind(pack_lon(fields, upstream, (near,) + rest, g_lower), "lon", -1)
    g_upper, w, gb1 = windows((1,), False, *shared, bias1, *rest, w)
    g_second, w, gb0, gb1, lon_back = windows(
        (0, 1), True, *shared, bias0, bias1, near, *rest, lon, w, gb0, gb1
    )
    keep, send = fold(w, gb0, gb1, target, core)
    half, other = reduce_slab(keep, send)
    lon_in = from_behind(lon_back, "lon", 1)
    own, lev_out, lat_out, diag_out = merge(g_lower, g_upper, g_second, lon_in)
    lev_in = from_behind(lev_out, "lev", 1)
    lat_in = from_behind(lat_out, "lat", 1)
    diag_in = from_corner(diag_out, 1)
    field_grad = place(own, lev_in, lat_in, diag_in)

    samples, levels, rows, cols, _ = fields.shape
    tokens = samples * levels * rows * cols
    for axis in ("lon", "lat", "lev"):
        tokens = tokens * lax.axis_size(axis)
    qkv_grad, out_grad, bias_grad = finish(half, other, core, 1.0 / math.sqrt(tokens))
    return (field_grad, qkv_grad, out_grad, bias_grad.transpose(0, 2, 1, 3))


def solution(mesh):
    return jax.shard_map(
        body,
        mesh=mesh,
        in_specs=(
            P(None, "lev", "lat", "lon", None),
            P(None, "lev", "lat", "lon", None),
            P(),
            P(),
            P("lev", "lat", None, None),
        ),
        out_specs=(P(None, "lev", "lat", "lon", None), P(), P(), P("lev", "lat", None, None)),
        check_vma=False,
    )
```

```python
import functools
import math

import jax
import jax.numpy as jnp
from jax import lax
from jax.experimental import pallas as pl
from jax.experimental.pallas import tpu as pltpu
from jax.sharding import PartitionSpec as P

HEADS = 6
WZ = 2
WH = 6
WW = 12
WIN = 144
PAIRS = 3312
C = 192
HD = 32
OFFS = 2 * WW - 1
GROUP = WH * OFFS
LANES = 384
KEYS = 256
NEG_FILL = -1e30
EPS = 1e-05
SCALE = HD**-0.5
SLAB = 1536
SIDE = SLAB // 2
WROWS = 1152
BF = jnp.bfloat16
F32 = jnp.float32
SPREAD = 896
MAIN = 128
TAIL = WIN - MAIN
TAILS = HEADS * MAIN
PAIR = 2 * WIN
BOTH = 2 * C
VMEM = pl.BlockSpec(memory_space=pltpu.VMEM)
HBM = pl.BlockSpec(memory_space=pl.ANY)
SMEM = pl.BlockSpec(memory_space=pltpu.SMEM)


def params(mib):
    return pltpu.CompilerParams(vmem_limit_bytes=mib * 1024 * 1024)


def cost(flops, nbytes):
    return pl.CostEstimate(flops=flops, bytes_accessed=nbytes, transcendentals=0)


def dot(a, b, ca=1, cb=0):
    return lax.dot_general(a, b, (((ca,), (cb,)), ((), ())), preferred_element_type=F32)


def shape(dims, dtype):
    return jax.ShapeDtypeStruct(dims, dtype)


def join(a, b):
    return jnp.concatenate([a[:, 0:128], b[:, 0:128], a[:, 128:C], b[:, 128:C]], axis=1)


def split(m):
    return (
        jnp.concatenate([m[:, 0:128], m[:, 256:320]], axis=1),
        jnp.concatenate([m[:, 128:256], m[:, 320:384]], axis=1),
    )


def both_lines(f, u, b, level, row):
    return join(f[b, level, row].astype(F32), u[b, level, row].astype(F32))


def pack_lev_kernel(f, u, out, tmp):
    for b in range(2):
        for r in range(9):
            tmp[b, r * 18 : r * 18 + 18, :] = both_lines(f, u, b, 0, r + 3)[6:24]
    out[...] = tmp[...].astype(BF)


def pack_lev(fields, upstream):
    return pl.pallas_call(
        pack_lev_kernel,
        name="pack_lev",
        out_shape=shape((2, 162, BOTH), BF),
        in_specs=[VMEM] * 2,
        out_specs=VMEM,
        scratch_shapes=[pltpu.VMEM((2, 162, BOTH), F32)],
        compiler_params=params(16),
        cost_estimate=cost(0, 2 * 1024 * 1024),
    )(fields, upstream)


def pack_lon_kernel(f, u, out, tmp):
    for b in range(2):
        for level in range(2):
            for row in range(12):
                at = (level * 12 + row) * 6
                tmp[b, at : at + 6, :] = both_lines(f, u, b, level, row)[0:6]
    out[...] = tmp[...].astype(BF)


def pack_lon(fields, upstream):
    return pl.pallas_call(
        pack_lon_kernel,
        name="pack_lon",
        out_shape=shape((2, WIN, BOTH), BF),
        in_specs=[VMEM] * 2,
        out_specs=VMEM,
        scratch_shapes=[pltpu.VMEM((2, WIN, BOTH), F32)],
        compiler_params=params(16),
        cost_estimate=cost(0, 2 * 1024 * 1024),
    )(fields, upstream)


def pack_rest_kernel(f, u, lon, diag, edge, lat):
    for b in range(2):
        halo = lon[b].astype(F32)
        for level, out in ((0, diag), (1, lat)):
            for row in range(3):
                at = (level * 12 + row) * 6
                line = both_lines(f, u, b, level, row)
                out[b, row] = jnp.concatenate([line[6:24], halo[at : at + 6]], axis=0).astype(BF)
        edge[b] = halo[18:72].astype(BF)


def pack_rest(fields, upstream, lon):
    return pl.pallas_call(
        pack_rest_kernel,
        name="pack_rest",
        out_shape=(
            shape((2, 3, 24, BOTH), BF), shape((2, 54, BOTH), BF), shape((2, 3, 24, BOTH), BF)
        ),
        in_specs=[VMEM] * 3,
        out_specs=(VMEM,) * 3,
        compiler_params=params(16),
        cost_estimate=cost(0, 2 * 1024 * 1024),
    )(fields, upstream, lon)


def onehot_rows(target, w1):
    row = lax.broadcasted_iota(jnp.int32, (KEYS, target.shape[1]), 0)
    return jnp.where(row == target + w1, 1.0, 0.0).astype(BF)


def expand_kernel(eb, target, region_k, region_q, out0, out1, spread, wide):
    spread[...] = jnp.zeros_like(spread)
    for z1 in range(2):
        for h1 in range(6):
            for z2 in range(2):
                off = ((z1 * 2 + z2) * 6 + h1) * GROUP
                for aw in range(2):
                    at = (z1 * 6 + h1) * 24 + (z2 * 2 + aw) * 6
                    spread[at : at + 6, 0:GROUP] = eb[0, aw, :, off : off + GROUP]
    full = spread[...]
    high = full.astype(BF)
    rest = full - high.astype(F32)
    mid = rest.astype(BF)
    low = (rest - mid.astype(F32)).astype(BF)
    tgt = target[...]
    for w1 in range(WW):
        hot = onehot_rows(tgt, w1)
        block = dot(high, hot) + (dot(mid, hot) + dot(low, hot))
        for g in range(12):
            wide[pl.ds(g * 12 + w1, 24, stride=WIN), :] = block[g * 24 : g * 24 + 24]
    for aw, out in enumerate((out0, out1)):
        for z2 in range(2):
            keys = slice(z2 * 72, z2 * 72 + 72)
            ok = region_k[aw, keys, :] == region_q[aw]
            tails = []
            for h in range(HEADS):
                at = ((z2 * 2 + aw) * HEADS + h) * WIN
                turned = wide[at : at + WIN, 0:72].T
                out[keys, h * MAIN : (h + 1) * MAIN] = jnp.where(
                    ok[:, 0:MAIN], turned[:, 0:MAIN], NEG_FILL
                )
                tails.append(turned[:, MAIN:WIN])
            tails.append(jnp.zeros((72, SPREAD - HEADS * WIN), F32))
            out[keys, TAILS:SPREAD] = jnp.where(
                ok[:, MAIN:], jnp.concatenate(tails, axis=1), NEG_FILL
            )


def expand(earth_bias, target, region_k, region_q):
    return pl.pallas_call(
        expand_kernel,
        name="expand_bias",
        out_shape=(shape((WIN, SPREAD), F32),) * 2,
        in_specs=[VMEM] * 4,
        out_specs=(VMEM,) * 2,
        scratch_shapes=[pltpu.VMEM((288, KEYS), F32), pltpu.VMEM((24 * WIN, 128), F32)],
        compiler_params=params(16),
        cost_estimate=cost(4 * 10**9, 4 * 1024 * 1024),
    )(earth_bias, target, region_k, region_q)


def windows_kernel(aw, seconds, *refs):
    refs = list(refs)
    take = lambda n: [refs.pop(0) for _ in range(n)]
    f, u, wqkv, wo, bias, inner = take(6)
    if aw == 1:
        lat, diag = take(2)
    if True in seconds:
        lon, edge = take(2)
        (w_in,) = take(1)
    (other,) = take(1) if True in seconds else (None,)
    grads, w_s, gb_s = take(3)
    if aw == 1:
        (lon_back,) = take(1)
    x_s, u_s, i_s, low_s, q_s, k_s, v_s, ga_s, gq_s, gk_s, gv_s, att_s, up_s = take(13)
    if aw == 1:
        g_s, lon_s = take(2)
    w_s[...] = w_in[...] if True in seconds else jnp.zeros_like(w_s)
    gb_s[...] = other[...] if aw == 0 and True in seconds else jnp.zeros_like(gb_s)

    def put(row, pair):
        for value, dst in zip(pair, (x_s, u_s)):
            dst[row : row + value.shape[0], :] = value

    for b in range(2):
        lines = inner[b].astype(F32)
        if True in seconds:
            at_lon, at_edge = lon[b].astype(F32), edge[b].astype(F32)
        for n, second in enumerate(seconds):
            for z in range(2):
                for h in range(6):
                    r = aw * 6 + h
                    row = (n * 2 + b) * WIN + z * 72 + h * 12
                    if r >= 9:
                        line = (diag if z else lat)[b, r - 9].astype(F32)
                        put(row, split(line[12:24] if second else line[0:12]))
                        continue
                    if z:
                        line = split(lines[r * 18 : r * 18 + 18])
                    else:
                        line = [a[b, 1, r + 3].astype(F32)[6:24] for a in (f, u)]
                    if second:
                        put(row, [a[12:18] for a in line])
                        halo = at_edge[r * 6 : r * 6 + 6] if z else at_lon[(r + 15) * 6 : (r + 16) * 6]
                        put(row + 6, split(halo))
                    else:
                        put(row, [a[0:12] for a in line])

    weights = wqkv[...].astype(F32)
    wq, wk, wv = [weights[:, i * C : (i + 1) * C].astype(BF) for i in range(3)]
    raw = x_s[...]
    centred = raw - jnp.mean(raw, axis=-1, keepdims=True)
    inv_std = lax.rsqrt(jnp.mean(centred * centred, axis=-1, keepdims=True) + EPS)
    normed = centred * inv_std
    low = normed.astype(BF)
    x_s[...] = normed
    i_s[...] = inv_std
    low_s[...] = low
    q_s[...] = dot(low, wq).astype(BF)
    k_s[...] = dot(low, wk).astype(BF)
    v_s[...] = dot(low, wv).astype(BF)
    up = u_s[...].astype(BF)
    ga_s[...] = dot(up, wo[...], 1, 1).astype(BF)
    att_s[...] = jnp.zeros_like(att_s)
    up_s[...] = jnp.zeros_like(up_s)
    for w in range(2 * len(seconds)):
        up_s[w * KEYS : w * KEYS + WIN, :] = up[w * WIN : (w + 1) * WIN]

    lane = lax.broadcasted_iota(jnp.int32, (1, C), 1)
    picks = [
        jnp.where((lane >= h * HD) & (lane < (h + 1) * HD), 1.0, 0.0).astype(BF)
        for h in range(HEADS)
    ]

    def stack(a):
        pad = jnp.zeros((SPREAD - HEADS * WIN, C), BF)
        mains = [a[0:MAIN] * m for m in picks]
        return jnp.concatenate(mains + [a[MAIN:WIN] * m for m in picks] + [pad], axis=0)

    def per_head(a, probs):
        tails = dot(a, probs[:, TAILS:SPREAD])
        heads = []
        for i in range(HEADS // 2):
            pair = dot(a[2 * i * HD : 2 * (i + 1) * HD], probs[:, 2 * i * MAIN : 2 * (i + 1) * MAIN])
            for n in range(2):
                h = 2 * i + n
                main = pair[n * HD : (n + 1) * HD, n * MAIN : (n + 1) * MAIN]
                tail = tails[h * HD : (h + 1) * HD, h * TAIL : (h + 1) * TAIL]
                heads.append(jnp.concatenate([main, tail], axis=1))
        return jnp.concatenate(heads, axis=0)

    for w in range(2 * len(seconds)):
        rows = slice(w * WIN, (w + 1) * WIN)
        low, q, k, v, ga = low_s[rows, :], q_s[rows, :], k_s[rows, :], v_s[rows, :], ga_s[rows, :]
        qs = stack(q)
        gas = stack(ga)
        scores = dot(k, qs, 1, 1)
        grad_probs = dot(v, gas, 1, 1)
        probs, grads_low = [], []
        for i in range(SPREAD // 128):
            cols = slice(i * 128, (i + 1) * 128)
            s = scores[:, cols] * SCALE + bias[:, cols]
            e = jnp.exp(s - jnp.max(s, axis=0, keepdims=True))
            p = e * (1.0 / jnp.sum(e, axis=0, keepdims=True))
            gp = grad_probs[:, cols]
            gs = p * (gp - jnp.sum(p * gp, axis=0, keepdims=True))
            gb_s[:, cols] += gs
            probs.append(p.astype(BF))
            grads_low.append(gs.astype(BF))
        p = jnp.concatenate(probs, axis=1)
        gs = jnp.concatenate(grads_low, axis=1)
        gv_s[rows, :] = dot(p, gas).astype(BF)
        gk_s[rows, :] = (dot(gs, qs) * SCALE).astype(BF)
        gq_s[rows, :] = (per_head(k.T, gs) * SCALE).T.astype(BF)
        att_s[:, w * KEYS : w * KEYS + WIN] = per_head(v.T, p).astype(BF)

    w_s[3 * C : 4 * C, :] += dot(att_s[...], up_s[...])
    gq, gk, gv = gq_s[...], gk_s[...], gv_s[...]
    low_t = low_s[...].T
    w_s[0:C, :] += dot(low_t, gq)
    w_s[C : 2 * C, :] += dot(low_t, gk)
    w_s[2 * C : 3 * C, :] += dot(low_t, gv)
    gu = dot(gq, wq, 1, 1) + dot(gk, wk, 1, 1) + dot(gv, wv, 1, 1)
    normed = x_s[...]
    centre = jnp.mean(gu, axis=-1, keepdims=True)
    along = jnp.mean(gu * normed, axis=-1, keepdims=True)
    grad = i_s[...] * (gu - centre - normed * along)
    grads[...] = grad.astype(BF)
    if aw == 0:
        return

    g_s[0:PAIR, :] = other[...].astype(F32)
    g_s[PAIR : 2 * PAIR, :] = grad[PAIR : 2 * PAIR]
    for b in range(2):
        for z in range(2):
            for r in range(12):
                row = ((r // 6) * 2 + b) * WIN + z * 72 + (r % 6) * 12
                to = b * WIN + (z * 12 + r) * 6
                lon_s[to : to + 6, :] = g_s[row + 6 : row + 12, :]
    lon_back[...] = lon_s[...].astype(BF)


def fold_kernel(w_s, gb0, gb1, target, core, keep, send, turned, slab):
    slab[0:768, :] = w_s[:, 0:128].astype(BF)
    slab[768:1152, :] = jnp.concatenate([w_s[0:384, 128:192], w_s[384:768, 128:192]], axis=1).astype(BF)
    for z2 in range(2):
        for aw, gb in enumerate((gb0, gb1)):
            rows = slice(z2 * 72, z2 * 72 + 72)
            tails = gb[rows, TAILS:SPREAD].T
            for h in range(HEADS):
                at = ((z2 * HEADS + h) * 2 + aw) * WIN
                turned[at : at + MAIN, 0:72] = gb[rows, h * MAIN : (h + 1) * MAIN].T
                turned[at + MAIN : at + WIN, 0:72] = tails[h * TAIL : (h + 1) * TAIL]
    folded = jnp.zeros((288, KEYS), F32)
    tgt = target[...]
    for w1 in range(WW):
        rows = [turned[pl.ds(g * 12 + w1, 24, stride=WIN), :] for g in range(12)]
        full = jnp.concatenate(rows, axis=0)[:, 0:72].astype(BF)
        hot = onehot_rows(tgt[:, 0:72], w1)
        folded = folded + dot(full, hot, 1, 1)
    slab[1152:1440, :] = folded[:, 0:128].astype(BF)
    rest = [folded[24 * i : 24 * i + 24, 128:138] for i in range(12)]
    rest = jnp.concatenate(rest + [jnp.zeros((24, 8), F32)], axis=1)
    slab[1440:1536, :] = jnp.concatenate([rest, jnp.zeros((72, 128), F32)], axis=0).astype(BF)
    top = pl.multiple_of(core[0, 0] * SIDE, SIDE)
    keep[...] = slab[pl.ds(top, SIDE), :]
    send[...] = slab[pl.ds(SIDE - top, SIDE), :]


def fold(w, gb0, gb1, target, core):
    return pl.pallas_call(
        fold_kernel,
        name="fold",
        out_shape=(shape((SIDE, 128), BF),) * 2,
        in_specs=[VMEM] * 4 + [SMEM],
        out_specs=(VMEM,) * 2,
        scratch_shapes=[
            pltpu.VMEM((24 * WIN, 128), F32),
            pltpu.VMEM((SLAB, 128), BF),
        ],
        compiler_params=params(24),
        cost_estimate=cost(2 * 10**9, 4 * 1024 * 1024),
    )(w, gb0, gb1, target, core)


def windows(aw, seconds, *args):
    tokens = len(seconds) * PAIR
    padded = 2 * len(seconds) * KEYS
    rows = [pltpu.VMEM((tokens, C), F32)] * 2 + [pltpu.VMEM((tokens, 1), F32)]
    rows += [pltpu.VMEM((tokens, C), BF)] * 8
    rows += [pltpu.VMEM((C, padded), BF), pltpu.VMEM((padded, C), BF)]
    outs = (shape((tokens, C), BF), shape((4 * C, C), F32), shape((WIN, SPREAD), F32))
    if aw == 1:
        outs += (shape((2 * WIN, C), BF),)
        rows += [pltpu.VMEM((2 * PAIR, C), F32), pltpu.VMEM((2 * WIN, C), F32)]
    return pl.pallas_call(
        functools.partial(windows_kernel, aw, seconds),
        name="windows_upper" if aw else "windows_lower_second" if seconds[0] else "windows_lower_first",
        out_shape=outs,
        in_specs=[VMEM] * len(args),
        out_specs=(VMEM,) * len(outs),
        scratch_shapes=rows,
        compiler_params=params(28),
        cost_estimate=cost(3 * 10**9 * len(seconds), 4 * 1024 * 1024),
    )(*args)


def merge_kernel(g_first, g_second, g_upper, lon_in, own, lev, lat, diag):
    for b in range(2):
        halo = lon_in[b * WIN : (b + 1) * WIN, :].astype(F32)
        for aw in range(2):
            at = slice(b * WIN, (b + 1) * WIN)
            after = slice(PAIR + b * WIN, PAIR + (b + 1) * WIN)
            first = (g_upper if aw else g_first)[at, :].astype(F32)
            second = (g_upper[after, :] if aw else g_second[at, :]).astype(F32)
            for z in range(2):
                for h in range(6):
                    r = aw * 6 + h
                    off = z * 72 + h * 12
                    hrow = (z * 12 + r) * 6
                    line = jnp.concatenate(
                        [halo[hrow : hrow + 6], first[off : off + 12], second[off : off + 6]], axis=0
                    ).astype(BF)
                    if z == 0:
                        if r < 9:
                            own[b, r] = line
                        else:
                            lat[b, r - 9] = line
                    elif r < 9:
                        lev[b, r] = line
                    else:
                        diag[b, r - 9] = line


def merge(*args):
    return pl.pallas_call(
        merge_kernel,
        name="merge_lon",
        out_shape=(
            shape((2, 9, 24, C), BF),
            shape((2, 9, 24, C), BF),
            shape((2, 3, 24, C), BF),
            shape((2, 3, 24, C), BF),
        ),
        in_specs=[VMEM] * 4,
        out_specs=(VMEM,) * 4,
        compiler_params=params(16),
        cost_estimate=cost(2 * 10**10, 2 * 1024 * 1024),
    )(*args)


def place_kernel(own, lev, lat, diag, out):
    for b in range(2):
        out[b, 1, 3:12] = own[b].astype(F32)
        out[b, 1, 0:3] = lat[b].astype(F32)
        out[b, 0, 3:12] = lev[b].astype(F32)
        out[b, 0, 0:3] = diag[b].astype(F32)


def place(own, lev, lat, diag):
    return pl.pallas_call(
        place_kernel,
        name="place_grad",
        out_shape=shape((2, 2, 12, 24, C), F32),
        in_specs=[VMEM] * 4,
        out_specs=VMEM,
        compiler_params=params(16),
        cost_estimate=cost(2 * 10**10, 2 * 1024 * 1024),
    )(own, lev, lat, diag)


def finish_kernel(factor, half, other, core, qkv, out, bias, slab):
    top = pl.multiple_of(core[0, 0] * SIDE, SIDE)
    slab[pl.ds(top, SIDE), :] = half[...].astype(F32)
    slab[pl.ds(SIDE - top, SIDE), :] = other[...].astype(F32)
    full = slab[...]
    right = full[768:1152]
    rest = jnp.concatenate([right[:, 0:64], right[:, 64:128]], axis=0)
    whole = jnp.concatenate([full[0:768], rest], axis=1) * factor
    for j in range(3):
        qkv[:, j * C : (j + 1) * C] = whole[j * C : (j + 1) * C]
    out[...] = whole[3 * C : 4 * C]
    tail = full[1440:1464]
    tail = jnp.concatenate([tail[:, 10 * i : 10 * i + 10] for i in range(12)], axis=0)
    pairs = jnp.concatenate([full[1152:1440], tail], axis=1)
    for z1 in range(2):
        for h1 in range(6):
            for z2 in range(2):
                off = ((z1 * 2 + z2) * 6 + h1) * GROUP
                at = (z1 * 6 + h1) * 24 + z2 * 12
                bias[0, :, :, off : off + GROUP] = pairs[at : at + 12].reshape(HEADS, 2, GROUP)


def finish(half, other, core, factor):
    return pl.pallas_call(
        functools.partial(finish_kernel, factor),
        name="finish_params",
        out_shape=(
            shape((C, 3 * C), F32),
            shape((C, C), F32),
            shape((1, HEADS, 2, PAIRS), F32),
        ),
        in_specs=[VMEM, VMEM, SMEM],
        out_specs=(VMEM,) * 3,
        scratch_shapes=[pltpu.VMEM((SLAB, 128), F32)],
        compiler_params=params(16),
        cost_estimate=cost(0, 2 * 1024 * 1024),
    )(half, other, core)


def from_behind(x, axis, by):
    devices = lax.axis_size(axis)
    return lax.ppermute(x, axis, [(i, (i + by) % devices) for i in range(devices)])


def from_corner(x, by):
    lats, levs = lax.axis_size("lat"), lax.axis_size("lev")
    pairs = [
        (a * levs + v, ((a + by) % lats) * levs + (v + by) % levs)
        for a in range(lats)
        for v in range(levs)
    ]
    return lax.ppermute(x, ("lat", "lev"), pairs)


def other_core(x):
    return lax.ppermute(x, "lon", [(i, i ^ 1) for i in range(lax.axis_size("lon"))])


def reduce_slab(keep, send):
    lons, lats, levs = (lax.axis_size(a) for a in ("lon", "lat", "lev"))
    depth = lons // 4
    rows = SIDE // depth
    along = [[4 * z + low for z in range(depth)] for low in range(4)]
    plane = [
        [((4 * z + 2 * y + c) * lats + a) * levs + v for y in range(2) for a in range(lats) for v in range(levs)]
        for z in range(depth)
        for c in range(2)
    ]
    half = (keep.astype(F32) + other_core(send).astype(F32)).astype(BF)
    pieces = lax.all_to_all(
        half.reshape(depth, rows, 128), "lon", 0, 0, axis_index_groups=along, tiled=True
    )
    mine = jnp.sum(pieces.astype(F32), axis=0).astype(BF)
    count = 2 * lats * levs
    every = lax.all_to_all(
        jnp.broadcast_to(mine[None], (count, rows, 128)),
        ("lon", "lat", "lev"), 0, 0, axis_index_groups=plane, tiled=True,
    )
    lon = lax.axis_index("lon")
    first = (lon % 2) * SIDE + (lon // 4) * rows
    spot = jnp.arange(count, dtype=jnp.int32) % (lats * levs)
    same = spot == lax.axis_index("lat") * levs + lax.axis_index("lev")
    picked = jnp.where(same | (first < WROWS), 1.0, 0.0).astype(F32)
    mine = jnp.sum(every.astype(F32) * picked[:, None, None], axis=0).astype(BF)
    half = lax.all_to_all(
        jnp.broadcast_to(mine[None], (depth, rows, 128)), "lon", 0, 0, axis_index_groups=along, tiled=True
    ).reshape(SIDE, 128)
    return half, other_core(half)


def body(fields, upstream, qkv_weight, out_weight, earth_bias):
    inner = from_behind(pack_lev(fields, upstream), "lev", -1)
    lon = from_behind(pack_lon(fields, upstream), "lon", -1)
    diag_msg, edge_msg, lat_msg = pack_rest(fields, upstream, lon)
    diag = from_corner(diag_msg, -1)
    edge = from_behind(edge_msg, "lev", -1)
    lat = from_behind(lat_msg, "lat", -1)

    key = jnp.arange(WIN, dtype=jnp.int32)
    target = (key // WW) * OFFS - key % WW + WW - 1
    target = target[None, :MAIN]
    last_lev = lax.axis_index("lev") == lax.axis_size("lev") - 1
    last_lat = lax.axis_index("lat") == lax.axis_size("lat") - 1
    lev_flag = ((key // 72) == 1) & last_lev
    lat_flag = ((key // WW) % WH >= WH // 2) & last_lat
    region = jnp.stack(
        [2 * lev_flag.astype(F32), 2 * lev_flag.astype(F32) + lat_flag.astype(F32)]
    )
    ends = jnp.tile(region[:, MAIN:], (1, HEADS))
    pad = jnp.zeros((2, SPREAD - HEADS * WIN), F32)
    along = jnp.concatenate([region[:, :MAIN], ends, pad], axis=1)
    bias0, bias1 = expand(earth_bias, target, region[:, :, None], along[:, None, :])
    core = (lax.axis_index("lon") % 2).astype(jnp.int32).reshape(1, 1)

    shared = (
        fields, upstream,
        qkv_weight, out_weight,
    )
    g_first, w, gb0 = windows(0, (False,), *shared, bias0, inner)
    g_second, w, gb0 = windows(0, (True,), *shared, bias0, inner, lon, edge, w, gb0)
    g_upper, w, gb1, lon_back = windows(
        1, (False, True), *shared, bias1, inner, lat, diag, lon, edge, w, g_second
    )
    keep, send = fold(w, gb0, gb1, target, core)
    half, other = reduce_slab(keep, send)
    lon_in = from_behind(lon_back, "lon", 1)
    own, lev_out, lat_out, diag_out = merge(g_first, g_second, g_upper, lon_in)
    lev_in = from_behind(lev_out, "lev", 1)
    lat_in = from_behind(lat_out, "lat", 1)
    diag_in = from_corner(diag_out, 1)
    field_grad = place(own, lev_in, lat_in, diag_in)

    samples, levels, rows, cols, _ = fields.shape
    tokens = samples * levels * rows * cols
    for axis in ("lon", "lat", "lev"):
        tokens = tokens * lax.axis_size(axis)
    qkv_grad, out_grad, bias_grad = finish(half, other, core, 1.0 / math.sqrt(tokens))
    return (field_grad, qkv_grad, out_grad, bias_grad.transpose(0, 2, 1, 3))


def solution(mesh):
    return jax.shard_map(
        body,
        mesh=mesh,
        in_specs=(
            P(None, "lev", "lat", "lon", None),
            P(None, "lev", "lat", "lon", None),
            P(),
            P(),
            P("lev", "lat", None, None),
        ),
        out_specs=(P(None, "lev", "lat", "lon", None), P(), P(), P("lev", "lat", None, None)),
        check_vma=False,
    )
```

```python
import functools
import math

import jax
import jax.numpy as jnp
from jax import lax
from jax.experimental import pallas as pl
from jax.experimental.pallas import tpu as pltpu
from jax.sharding import PartitionSpec as P

HEADS = 6
WZ = 2
WH = 6
WW = 12
WIN = 144
PAIRS = 3312
C = 192
HD = 32
OFFS = 2 * WW - 1
GROUP = WH * OFFS
LANES = 384
KEYS = 256
NEG_FILL = -1e30
EPS = 1e-05
SCALE = HD**-0.5
SLAB = 1536
SIDE = SLAB // 2
WROWS = 1152
BF = jnp.bfloat16
F32 = jnp.float32
SPREAD = 896
MAIN = 128
TAIL = WIN - MAIN
TAILS = HEADS * MAIN
PAIR = 2 * WIN
BOTH = 2 * C
SPARE = 8
VMEM = pl.BlockSpec(memory_space=pltpu.VMEM)
HBM = pl.BlockSpec(memory_space=pl.ANY)
SMEM = pl.BlockSpec(memory_space=pltpu.SMEM)


def params(mib):
    return pltpu.CompilerParams(vmem_limit_bytes=mib * 1024 * 1024)


def cost(flops, nbytes):
    return pl.CostEstimate(flops=flops, bytes_accessed=nbytes, transcendentals=0)


def dot(a, b, ca=1, cb=0):
    return lax.dot_general(a, b, (((ca,), (cb,)), ((), ())), preferred_element_type=F32)


def shape(dims, dtype):
    return jax.ShapeDtypeStruct(dims, dtype)


def join(a, b):
    return jnp.concatenate([a[:, 0:128], b[:, 0:128], a[:, 128:C], b[:, 128:C]], axis=1)


def split(m):
    return (
        jnp.concatenate([m[:, 0:128], m[:, 256:320]], axis=1),
        jnp.concatenate([m[:, 128:256], m[:, 320:384]], axis=1),
    )


def both_lines(f, u, b, level, row):
    return join(f[b, level, row].astype(F32), u[b, level, row].astype(F32))


def pack_lev_kernel(f, u, out, tmp):
    for b in range(2):
        for r in range(9):
            tmp[b, r * 18 : r * 18 + 18, :] = both_lines(f, u, b, 0, r + 3)[6:24]
    out[...] = tmp[:, 0 : out.shape[1], :].astype(BF)


def pack_lev(fields, upstream):
    return pl.pallas_call(
        pack_lev_kernel,
        name="pack_lev",
        out_shape=shape((2, 162, BOTH), BF),
        in_specs=[VMEM] * 2,
        out_specs=VMEM,
        scratch_shapes=[pltpu.VMEM((2, 168 + SPARE, BOTH), F32)],
        compiler_params=params(16),
        cost_estimate=cost(0, 2 * 1024 * 1024),
    )(fields, upstream)


def pack_lon_kernel(f, u, out, tmp):
    for b in range(2):
        for level in range(2):
            for row in range(12):
                at = (level * 12 + row) * 6
                tmp[b, at : at + 6, :] = both_lines(f, u, b, level, row)[0:6]
    out[...] = tmp[:, 0 : out.shape[1], :].astype(BF)


def pack_lon(fields, upstream):
    return pl.pallas_call(
        pack_lon_kernel,
        name="pack_lon",
        out_shape=shape((2, WIN, BOTH), BF),
        in_specs=[VMEM] * 2,
        out_specs=VMEM,
        scratch_shapes=[pltpu.VMEM((2, WIN + SPARE, BOTH), F32)],
        compiler_params=params(16),
        cost_estimate=cost(0, 2 * 1024 * 1024),
    )(fields, upstream)


def pack_rest_kernel(f, u, lon, diag, edge, lat):
    for b in range(2):
        halo = lon[b].astype(F32)
        for level, out in ((0, diag), (1, lat)):
            for row in range(3):
                at = (level * 12 + row) * 6
                line = both_lines(f, u, b, level, row)
                out[b, row] = jnp.concatenate([line[6:24], halo[at : at + 6]], axis=0).astype(BF)
        edge[b] = halo[18:72].astype(BF)


def pack_rest(fields, upstream, lon):
    return pl.pallas_call(
        pack_rest_kernel,
        name="pack_rest",
        out_shape=(
            shape((2, 3, 24, BOTH), BF), shape((2, 54, BOTH), BF), shape((2, 3, 24, BOTH), BF)
        ),
        in_specs=[VMEM] * 3,
        out_specs=(VMEM,) * 3,
        compiler_params=params(16),
        cost_estimate=cost(0, 2 * 1024 * 1024),
    )(fields, upstream, lon)


def onehot_rows(target, w1):
    row = lax.broadcasted_iota(jnp.int32, (KEYS, target.shape[1]), 0)
    return jnp.where(row == target + w1, 1.0, 0.0).astype(BF)


def expand_kernel(eb, target, region_k, region_q, out0, out1, spread, wide):
    spread[...] = jnp.zeros_like(spread)
    for z1 in range(2):
        for h1 in range(6):
            for z2 in range(2):
                off = ((z1 * 2 + z2) * 6 + h1) * GROUP
                for aw in range(2):
                    at = (z1 * 6 + h1) * 24 + (z2 * 2 + aw) * 6
                    spread[at : at + 6, 0:GROUP] = eb[0, aw, :, off : off + GROUP]
    full = spread[0:288, :]
    high = full.astype(BF)
    rest = full - high.astype(F32)
    mid = rest.astype(BF)
    low = (rest - mid.astype(F32)).astype(BF)
    tgt = target[...]
    for w1 in range(WW):
        hot = onehot_rows(tgt, w1)
        block = dot(high, hot) + (dot(mid, hot) + dot(low, hot))
        for g in range(12):
            wide[pl.ds(g * 12 + w1, 24, stride=WIN), :] = block[g * 24 : g * 24 + 24]
    for aw, out in enumerate((out0, out1)):
        for z2 in range(2):
            keys = slice(z2 * 72, z2 * 72 + 72)
            ok = region_k[aw, keys, :] == region_q[aw]
            tails = []
            for h in range(HEADS):
                at = ((z2 * 2 + aw) * HEADS + h) * WIN
                turned = wide[at : at + WIN, 0:72].T
                out[keys, h * MAIN : (h + 1) * MAIN] = jnp.where(
                    ok[:, 0:MAIN], turned[:, 0:MAIN], NEG_FILL
                )
                tails.append(turned[:, MAIN:WIN])
            tails.append(jnp.zeros((72, SPREAD - HEADS * WIN), F32))
            out[keys, TAILS:SPREAD] = jnp.where(
                ok[:, MAIN:], jnp.concatenate(tails, axis=1), NEG_FILL
            )


def expand(earth_bias, target, region_k, region_q):
    return pl.pallas_call(
        expand_kernel,
        name="expand_bias",
        out_shape=(shape((WIN, SPREAD), F32),) * 2,
        in_specs=[VMEM] * 4,
        out_specs=(VMEM,) * 2,
        scratch_shapes=[pltpu.VMEM((288 + SPARE, KEYS), F32), pltpu.VMEM((25 * WIN, 128), F32)],
        compiler_params=params(16),
        cost_estimate=cost(4 * 10**9, 4 * 1024 * 1024),
    )(earth_bias, target, region_k, region_q)


def windows_kernel(aw, seconds, *refs):
    refs = list(refs)
    take = lambda n: [refs.pop(0) for _ in range(n)]
    f, u, wqkv, wo, bias, inner = take(6)
    if aw == 1:
        lat, diag = take(2)
    if True in seconds:
        lon, edge = take(2)
        (w_in,) = take(1)
    (other,) = take(1) if True in seconds else (None,)
    grads, w_s, gb_s = take(3)
    if aw == 1:
        (lon_back,) = take(1)
    x_s, u_s, i_s, low_s, q_s, k_s, v_s, ga_s, gq_s, gk_s, gv_s, att_s, up_s = take(13)
    if aw == 1:
        g_s, lon_s = take(2)
    w_s[...] = w_in[...] if True in seconds else jnp.zeros_like(w_s)
    gb_s[...] = other[...] if aw == 0 and True in seconds else jnp.zeros_like(gb_s)

    def put(row, pair):
        for value, dst in zip(pair, (x_s, u_s)):
            dst[row : row + value.shape[0], :] = value

    for b in range(2):
        lines = inner[b].astype(F32)
        if True in seconds:
            at_lon, at_edge = lon[b].astype(F32), edge[b].astype(F32)
        for n, second in enumerate(seconds):
            for z in range(2):
                for h in range(6):
                    r = aw * 6 + h
                    row = (n * 2 + b) * WIN + z * 72 + h * 12
                    if r >= 9:
                        line = (diag if z else lat)[b, r - 9].astype(F32)
                        put(row, split(line[12:24] if second else line[0:12]))
                        continue
                    if z:
                        line = split(lines[r * 18 : r * 18 + 18])
                    else:
                        line = [a[b, 1, r + 3].astype(F32)[6:24] for a in (f, u)]
                    if second:
                        put(row, [a[12:18] for a in line])
                        halo = at_edge[r * 6 : r * 6 + 6] if z else at_lon[(r + 15) * 6 : (r + 16) * 6]
                        put(row + 6, split(halo))
                    else:
                        put(row, [a[0:12] for a in line])

    weights = wqkv[...].astype(F32)
    wq, wk, wv = [weights[:, i * C : (i + 1) * C].astype(BF) for i in range(3)]
    tokens = len(seconds) * PAIR
    raw = x_s[0:tokens, :]
    centred = raw - jnp.mean(raw, axis=-1, keepdims=True)
    inv_std = lax.rsqrt(jnp.mean(centred * centred, axis=-1, keepdims=True) + EPS)
    normed = centred * inv_std
    low = normed.astype(BF)
    x_s[0:tokens, :] = normed
    i_s[...] = inv_std
    low_s[...] = low
    q_s[...] = dot(low, wq).astype(BF)
    k_s[...] = dot(low, wk).astype(BF)
    v_s[...] = dot(low, wv).astype(BF)
    up = u_s[0:tokens, :].astype(BF)
    ga_s[...] = dot(up, wo[...], 1, 1).astype(BF)
    att_s[...] = jnp.zeros_like(att_s)
    up_s[...] = jnp.zeros_like(up_s)
    for w in range(2 * len(seconds)):
        up_s[w * KEYS : w * KEYS + WIN, :] = up[w * WIN : (w + 1) * WIN]

    lane = lax.broadcasted_iota(jnp.int32, (1, C), 1)
    picks = [
        jnp.where((lane >= h * HD) & (lane < (h + 1) * HD), 1.0, 0.0).astype(BF)
        for h in range(HEADS)
    ]

    def stack(a):
        pad = jnp.zeros((SPREAD - HEADS * WIN, C), BF)
        mains = [a[0:MAIN] * m for m in picks]
        return jnp.concatenate(mains + [a[MAIN:WIN] * m for m in picks] + [pad], axis=0)

    def per_head(a, probs):
        tails = dot(a, probs[:, TAILS:SPREAD])
        heads = []
        for i in range(HEADS // 2):
            pair = dot(a[2 * i * HD : 2 * (i + 1) * HD], probs[:, 2 * i * MAIN : 2 * (i + 1) * MAIN])
            for n in range(2):
                h = 2 * i + n
                main = pair[n * HD : (n + 1) * HD, n * MAIN : (n + 1) * MAIN]
                tail = tails[h * HD : (h + 1) * HD, h * TAIL : (h + 1) * TAIL]
                heads.append(jnp.concatenate([main, tail], axis=1))
        return jnp.concatenate(heads, axis=0)

    for w in range(2 * len(seconds)):
        rows = slice(w * WIN, (w + 1) * WIN)
        low, q, k, v, ga = low_s[rows, :], q_s[rows, :], k_s[rows, :], v_s[rows, :], ga_s[rows, :]
        qs = stack(q)
        gas = stack(ga)
        scores = dot(k, qs, 1, 1)
        grad_probs = dot(v, gas, 1, 1)
        probs, grads_low = [], []
        for i in range(SPREAD // 128):
            cols = slice(i * 128, (i + 1) * 128)
            s = scores[:, cols] * SCALE + bias[:, cols]
            e = jnp.exp(s - jnp.max(s, axis=0, keepdims=True))
            p = e * (1.0 / jnp.sum(e, axis=0, keepdims=True))
            gp = grad_probs[:, cols]
            gs = p * (gp - jnp.sum(p * gp, axis=0, keepdims=True))
            gb_s[:, cols] += gs
            probs.append(p.astype(BF))
            grads_low.append(gs.astype(BF))
        p = jnp.concatenate(probs, axis=1)
        gs = jnp.concatenate(grads_low, axis=1)
        gv_s[rows, :] = dot(p, gas).astype(BF)
        gk_s[rows, :] = (dot(gs, qs) * SCALE).astype(BF)
        gq_s[rows, :] = (per_head(k.T, gs) * SCALE).T.astype(BF)
        att_s[:, w * KEYS : w * KEYS + WIN] = per_head(v.T, p).astype(BF)

    w_s[3 * C : 4 * C, :] += dot(att_s[...], up_s[...])
    gq, gk, gv = gq_s[...], gk_s[...], gv_s[...]
    low_t = low_s[...].T
    w_s[0:C, :] += dot(low_t, gq)
    w_s[C : 2 * C, :] += dot(low_t, gk)
    w_s[2 * C : 3 * C, :] += dot(low_t, gv)
    gu = dot(gq, wq, 1, 1) + dot(gk, wk, 1, 1) + dot(gv, wv, 1, 1)
    normed = x_s[0:tokens, :]
    centre = jnp.mean(gu, axis=-1, keepdims=True)
    along = jnp.mean(gu * normed, axis=-1, keepdims=True)
    grad = i_s[...] * (gu - centre - normed * along)
    grads[...] = grad.astype(BF)
    if aw == 0:
        return

    g_s[0:PAIR, :] = other[...].astype(F32)
    g_s[PAIR : 2 * PAIR, :] = grad[PAIR : 2 * PAIR]
    for b in range(2):
        for z in range(2):
            for r in range(12):
                row = ((r // 6) * 2 + b) * WIN + z * 72 + (r % 6) * 12
                to = b * WIN + (z * 12 + r) * 6
                lon_s[to : to + 6, :] = g_s[row + 6 : row + 12, :]
    lon_back[...] = lon_s[0 : 2 * WIN, :].astype(BF)


def fold_kernel(w_s, gb0, gb1, target, core, keep, send, turned, slab):
    slab[0:768, :] = w_s[:, 0:128].astype(BF)
    slab[768:1152, :] = jnp.concatenate([w_s[0:384, 128:192], w_s[384:768, 128:192]], axis=1).astype(BF)
    for z2 in range(2):
        for aw, gb in enumerate((gb0, gb1)):
            rows = slice(z2 * 72, z2 * 72 + 72)
            tails = gb[rows, TAILS:SPREAD].T
            for h in range(HEADS):
                at = ((z2 * HEADS + h) * 2 + aw) * WIN
                turned[at : at + MAIN, 0:72] = gb[rows, h * MAIN : (h + 1) * MAIN].T
                turned[at + MAIN : at + WIN, 0:72] = tails[h * TAIL : (h + 1) * TAIL]
    folded = jnp.zeros((288, KEYS), F32)
    tgt = target[...]
    for w1 in range(WW):
        rows = [turned[pl.ds(g * 12 + w1, 24, stride=WIN), :] for g in range(12)]
        full = jnp.concatenate(rows, axis=0)[:, 0:72].astype(BF)
        hot = onehot_rows(tgt[:, 0:72], w1)
        folded = folded + dot(full, hot, 1, 1)
    slab[1152:1440, :] = folded[:, 0:128].astype(BF)
    rest = [folded[24 * i : 24 * i + 24, 128:138] for i in range(12)]
    rest = jnp.concatenate(rest + [jnp.zeros((24, 8), F32)], axis=1)
    slab[1440:1536, :] = jnp.concatenate([rest, jnp.zeros((72, 128), F32)], axis=0).astype(BF)
    top = pl.multiple_of(core[0, 0] * SIDE, SIDE)
    keep[...] = slab[pl.ds(top, SIDE), :]
    send[...] = slab[pl.ds(SIDE - top, SIDE), :]


def fold(w, gb0, gb1, target, core):
    return pl.pallas_call(
        fold_kernel,
        name="fold",
        out_shape=(shape((SIDE, 128), BF),) * 2,
        in_specs=[VMEM] * 4 + [SMEM],
        out_specs=(VMEM,) * 2,
        scratch_shapes=[
            pltpu.VMEM((25 * WIN, 128), F32),
            pltpu.VMEM((SLAB, 128), BF),
        ],
        compiler_params=params(24),
        cost_estimate=cost(2 * 10**9, 4 * 1024 * 1024),
    )(w, gb0, gb1, target, core)


def windows(aw, seconds, *args):
    tokens = len(seconds) * PAIR
    padded = 2 * len(seconds) * KEYS
    rows = [pltpu.VMEM((tokens + SPARE, C), F32)] * 2 + [pltpu.VMEM((tokens, 1), F32)]
    rows += [pltpu.VMEM((tokens, C), BF)] * 8
    rows += [pltpu.VMEM((C, padded), BF), pltpu.VMEM((padded, C), BF)]
    outs = (shape((tokens, C), BF), shape((4 * C, C), F32), shape((WIN, SPREAD), F32))
    if aw == 1:
        outs += (shape((2 * WIN, C), BF),)
        rows += [pltpu.VMEM((2 * PAIR + SPARE, C), F32), pltpu.VMEM((2 * WIN + SPARE, C), F32)]
    return pl.pallas_call(
        functools.partial(windows_kernel, aw, seconds),
        name="windows_upper" if aw else "windows_lower_second" if seconds[0] else "windows_lower_first",
        out_shape=outs,
        in_specs=[VMEM] * len(args),
        out_specs=(VMEM,) * len(outs),
        scratch_shapes=rows,
        compiler_params=params(28),
        cost_estimate=cost(3 * 10**9 * len(seconds), 4 * 1024 * 1024),
    )(*args)


def merge_kernel(g_first, g_second, g_upper, lon_in, own, lev, lat, diag):
    for b in range(2):
        halo = lon_in[b * WIN : (b + 1) * WIN, :].astype(F32)
        for aw in range(2):
            at = slice(b * WIN, (b + 1) * WIN)
            after = slice(PAIR + b * WIN, PAIR + (b + 1) * WIN)
            first = (g_upper if aw else g_first)[at, :].astype(F32)
            second = (g_upper[after, :] if aw else g_second[at, :]).astype(F32)
            for z in range(2):
                for h in range(6):
                    r = aw * 6 + h
                    off = z * 72 + h * 12
                    hrow = (z * 12 + r) * 6
                    line = jnp.concatenate(
                        [halo[hrow : hrow + 6], first[off : off + 12], second[off : off + 6]], axis=0
                    ).astype(BF)
                    if z == 0:
                        if r < 9:
                            own[b, r] = line
                        else:
                            lat[b, r - 9] = line
                    elif r < 9:
                        lev[b, r] = line
                    else:
                        diag[b, r - 9] = line


def merge(*args):
    return pl.pallas_call(
        merge_kernel,
        name="merge_lon",
        out_shape=(
            shape((2, 9, 24, C), BF),
            shape((2, 9, 24, C), BF),
            shape((2, 3, 24, C), BF),
            shape((2, 3, 24, C), BF),
        ),
        in_specs=[VMEM] * 4,
        out_specs=(VMEM,) * 4,
        compiler_params=params(16),
        cost_estimate=cost(2 * 10**10, 2 * 1024 * 1024),
    )(*args)


def place_kernel(own, lev, lat, diag, out):
    for b in range(2):
        out[b, 1, 3:12] = own[b].astype(F32)
        out[b, 1, 0:3] = lat[b].astype(F32)
        out[b, 0, 3:12] = lev[b].astype(F32)
        out[b, 0, 0:3] = diag[b].astype(F32)


def place(own, lev, lat, diag):
    return pl.pallas_call(
        place_kernel,
        name="place_grad",
        out_shape=shape((2, 2, 12, 24, C), F32),
        in_specs=[VMEM] * 4,
        out_specs=VMEM,
        compiler_params=params(16),
        cost_estimate=cost(2 * 10**10, 2 * 1024 * 1024),
    )(own, lev, lat, diag)


def finish_kernel(factor, half, other, core, qkv, out, bias, slab):
    top = pl.multiple_of(core[0, 0] * SIDE, SIDE)
    slab[pl.ds(top, SIDE), :] = half[...].astype(F32)
    slab[pl.ds(SIDE - top, SIDE), :] = other[...].astype(F32)
    full = slab[...]
    right = full[768:1152]
    rest = jnp.concatenate([right[:, 0:64], right[:, 64:128]], axis=0)
    whole = jnp.concatenate([full[0:768], rest], axis=1) * factor
    for j in range(3):
        qkv[:, j * C : (j + 1) * C] = whole[j * C : (j + 1) * C]
    out[...] = whole[3 * C : 4 * C]
    tail = full[1440:1464]
    tail = jnp.concatenate([tail[:, 10 * i : 10 * i + 10] for i in range(12)], axis=0)
    pairs = jnp.concatenate([full[1152:1440], tail], axis=1)
    for z1 in range(2):
        for h1 in range(6):
            for z2 in range(2):
                off = ((z1 * 2 + z2) * 6 + h1) * GROUP
                at = (z1 * 6 + h1) * 24 + z2 * 12
                bias[0, :, :, off : off + GROUP] = pairs[at : at + 12].reshape(HEADS, 2, GROUP)


def finish(half, other, core, factor):
    return pl.pallas_call(
        functools.partial(finish_kernel, factor),
        name="finish_params",
        out_shape=(
            shape((C, 3 * C), F32),
            shape((C, C), F32),
            shape((1, HEADS, 2, PAIRS), F32),
        ),
        in_specs=[VMEM, VMEM, SMEM],
        out_specs=(VMEM,) * 3,
        scratch_shapes=[pltpu.VMEM((SLAB, 128), F32)],
        compiler_params=params(16),
        cost_estimate=cost(0, 2 * 1024 * 1024),
    )(half, other, core)


def from_behind(x, axis, by):
    devices = lax.axis_size(axis)
    return lax.ppermute(x, axis, [(i, (i + by) % devices) for i in range(devices)])


def from_corner(x, by):
    lats, levs = lax.axis_size("lat"), lax.axis_size("lev")
    pairs = [
        (a * levs + v, ((a + by) % lats) * levs + (v + by) % levs)
        for a in range(lats)
        for v in range(levs)
    ]
    return lax.ppermute(x, ("lat", "lev"), pairs)


def other_core(x):
    return lax.ppermute(x, "lon", [(i, i ^ 1) for i in range(lax.axis_size("lon"))])


def reduce_slab(keep, send):
    lons, lats, levs = (lax.axis_size(a) for a in ("lon", "lat", "lev"))
    depth = lons // 4
    rows = SIDE // depth
    along = [[4 * z + low for z in range(depth)] for low in range(4)]
    plane = [
        [((4 * z + 2 * y + c) * lats + a) * levs + v for y in range(2) for a in range(lats) for v in range(levs)]
        for z in range(depth)
        for c in range(2)
    ]
    half = (keep.astype(F32) + other_core(send).astype(F32)).astype(BF)
    pieces = lax.all_to_all(
        half.reshape(depth, rows, 128), "lon", 0, 0, axis_index_groups=along, tiled=True
    )
    mine = jnp.sum(pieces.astype(F32), axis=0).astype(BF)
    count = 2 * lats * levs
    every = lax.all_to_all(
        jnp.broadcast_to(mine[None], (count, rows, 128)),
        ("lon", "lat", "lev"), 0, 0, axis_index_groups=plane, tiled=True,
    )
    lon = lax.axis_index("lon")
    first = (lon % 2) * SIDE + (lon // 4) * rows
    spot = jnp.arange(count, dtype=jnp.int32) % (lats * levs)
    same = spot == lax.axis_index("lat") * levs + lax.axis_index("lev")
    picked = jnp.where(same | (first < WROWS), 1.0, 0.0).astype(F32)
    mine = jnp.sum(every.astype(F32) * picked[:, None, None], axis=0).astype(BF)
    half = lax.all_to_all(
        jnp.broadcast_to(mine[None], (depth, rows, 128)), "lon", 0, 0, axis_index_groups=along, tiled=True
    ).reshape(SIDE, 128)
    return half, other_core(half)


def body(fields, upstream, qkv_weight, out_weight, earth_bias):
    inner = from_behind(pack_lev(fields, upstream), "lev", -1)
    lon = from_behind(pack_lon(fields, upstream), "lon", -1)
    diag_msg, edge_msg, lat_msg = pack_rest(fields, upstream, lon)
    diag = from_corner(diag_msg, -1)
    edge = from_behind(edge_msg, "lev", -1)
    lat = from_behind(lat_msg, "lat", -1)

    key = jnp.arange(WIN, dtype=jnp.int32)
    target = (key // WW) * OFFS - key % WW + WW - 1
    target = target[None, :MAIN]
    last_lev = lax.axis_index("lev") == lax.axis_size("lev") - 1
    last_lat = lax.axis_index("lat") == lax.axis_size("lat") - 1
    lev_flag = ((key // 72) == 1) & last_lev
    lat_flag = ((key // WW) % WH >= WH // 2) & last_lat
    region = jnp.stack(
        [2 * lev_flag.astype(F32), 2 * lev_flag.astype(F32) + lat_flag.astype(F32)]
    )
    ends = jnp.tile(region[:, MAIN:], (1, HEADS))
    pad = jnp.zeros((2, SPREAD - HEADS * WIN), F32)
    along = jnp.concatenate([region[:, :MAIN], ends, pad], axis=1)
    bias0, bias1 = expand(earth_bias, target, region[:, :, None], along[:, None, :])
    core = (lax.axis_index("lon") % 2).astype(jnp.int32).reshape(1, 1)

    shared = (
        fields, upstream,
        qkv_weight, out_weight,
    )
    g_first, w, gb0 = windows(0, (False,), *shared, bias0, inner)
    g_second, w, gb0 = windows(0, (True,), *shared, bias0, inner, lon, edge, w, gb0)
    g_upper, w, gb1, lon_back = windows(
        1, (False, True), *shared, bias1, inner, lat, diag, lon, edge, w, g_second
    )
    keep, send = fold(w, gb0, gb1, target, core)
    half, other = reduce_slab(keep, send)
    lon_in = from_behind(lon_back, "lon", 1)
    own, lev_out, lat_out, diag_out = merge(g_first, g_second, g_upper, lon_in)
    lev_in = from_behind(lev_out, "lev", 1)
    lat_in = from_behind(lat_out, "lat", 1)
    diag_in = from_corner(diag_out, 1)
    field_grad = place(own, lev_in, lat_in, diag_in)

    samples, levels, rows, cols, _ = fields.shape
    tokens = samples * levels * rows * cols
    for axis in ("lon", "lat", "lev"):
        tokens = tokens * lax.axis_size(axis)
    qkv_grad, out_grad, bias_grad = finish(half, other, core, 1.0 / math.sqrt(tokens))
    return (field_grad, qkv_grad, out_grad, bias_grad.transpose(0, 2, 1, 3))


def solution(mesh):
    return jax.shard_map(
        body,
        mesh=mesh,
        in_specs=(
            P(None, "lev", "lat", "lon", None),
            P(None, "lev", "lat", "lon", None),
            P(),
            P(),
            P("lev", "lat", None, None),
        ),
        out_specs=(P(None, "lev", "lat", "lon", None), P(), P(), P("lev", "lat", None, None)),
        check_vma=False,
    )
```

```python
import functools
import math

import jax
import jax.numpy as jnp
from jax import lax
from jax.experimental import pallas as pl
from jax.experimental.pallas import tpu as pltpu
from jax.sharding import PartitionSpec as P

HEADS = 6
WZ = 2
WH = 6
WW = 12
WIN = 144
PAIRS = 3312
C = 192
HD = 32
OFFS = 2 * WW - 1
GROUP = WH * OFFS
LANES = 384
KEYS = 256
NEG_FILL = -1e30
EPS = 1e-05
SCALE = HD**-0.5
SLAB = 1536
SIDE = SLAB // 2
WROWS = 1152
BF = jnp.bfloat16
F32 = jnp.float32
SPREAD = 896
MAIN = 128
TAIL = WIN - MAIN
TAILS = HEADS * MAIN
PAIR = 2 * WIN
BOTH = 2 * C
SPARE = 8
VMEM = pl.BlockSpec(memory_space=pltpu.VMEM)
HBM = pl.BlockSpec(memory_space=pl.ANY)
SMEM = pl.BlockSpec(memory_space=pltpu.SMEM)


def params(mib):
    return pltpu.CompilerParams(vmem_limit_bytes=mib * 1024 * 1024)


def cost(flops, nbytes):
    return pl.CostEstimate(flops=flops, bytes_accessed=nbytes, transcendentals=0)


def dot(a, b, ca=1, cb=0):
    return lax.dot_general(a, b, (((ca,), (cb,)), ((), ())), preferred_element_type=F32)


def shape(dims, dtype):
    return jax.ShapeDtypeStruct(dims, dtype)


def join(a, b):
    return jnp.concatenate([a[:, 0:128], b[:, 0:128], a[:, 128:C], b[:, 128:C]], axis=1)


def split(m):
    return (
        jnp.concatenate([m[:, 0:128], m[:, 256:320]], axis=1),
        jnp.concatenate([m[:, 128:256], m[:, 320:384]], axis=1),
    )


def both_lines(f, u, b, level, row):
    return join(f[b, level, row].astype(F32), u[b, level, row].astype(F32))


def pack_lev_kernel(f, u, out, tmp):
    for b in range(2):
        for r in range(9):
            tmp[b, r * 18 : r * 18 + 18, :] = both_lines(f, u, b, 0, r + 3)[6:24]
    out[...] = tmp[:, 0 : out.shape[1], :].astype(BF)


def pack_lev(fields, upstream):
    return pl.pallas_call(
        pack_lev_kernel,
        name="pack_lev",
        out_shape=shape((2, 162, BOTH), BF),
        in_specs=[VMEM] * 2,
        out_specs=VMEM,
        scratch_shapes=[pltpu.VMEM((2, 168 + SPARE, BOTH), F32)],
        compiler_params=params(16),
        cost_estimate=cost(0, 2 * 1024 * 1024),
    )(fields, upstream)


def pack_lon_kernel(f, u, out, tmp):
    for b in range(2):
        for level in range(2):
            for row in range(12):
                at = (level * 12 + row) * 6
                tmp[b, at : at + 6, :] = both_lines(f, u, b, level, row)[0:6]
    out[...] = tmp[:, 0 : out.shape[1], :].astype(BF)


def pack_lon(fields, upstream):
    return pl.pallas_call(
        pack_lon_kernel,
        name="pack_lon",
        out_shape=shape((2, WIN, BOTH), BF),
        in_specs=[VMEM] * 2,
        out_specs=VMEM,
        scratch_shapes=[pltpu.VMEM((2, WIN + SPARE, BOTH), F32)],
        compiler_params=params(16),
        cost_estimate=cost(0, 2 * 1024 * 1024),
    )(fields, upstream)


def pack_rest_kernel(f, u, lon, diag, edge, lat):
    for b in range(2):
        halo = lon[b].astype(F32)
        for level, out in ((0, diag), (1, lat)):
            for row in range(3):
                at = (level * 12 + row) * 6
                line = both_lines(f, u, b, level, row)
                out[b, row] = jnp.concatenate([line[6:24], halo[at : at + 6]], axis=0).astype(BF)
        edge[b] = halo[18:72].astype(BF)


def pack_rest(fields, upstream, lon):
    return pl.pallas_call(
        pack_rest_kernel,
        name="pack_rest",
        out_shape=(
            shape((2, 3, 24, BOTH), BF), shape((2, 54, BOTH), BF), shape((2, 3, 24, BOTH), BF)
        ),
        in_specs=[VMEM] * 3,
        out_specs=(VMEM,) * 3,
        compiler_params=params(16),
        cost_estimate=cost(0, 2 * 1024 * 1024),
    )(fields, upstream, lon)


def onehot_rows(target, w1):
    row = lax.broadcasted_iota(jnp.int32, (KEYS, target.shape[1]), 0)
    return jnp.where(row == target + w1, 1.0, 0.0).astype(BF)


def expand_kernel(eb, target, region_k, region_q, out0, out1, spread, wide):
    spread[...] = jnp.zeros_like(spread)
    for z1 in range(2):
        for h1 in range(6):
            for z2 in range(2):
                off = ((z1 * 2 + z2) * 6 + h1) * GROUP
                for aw in range(2):
                    at = (z1 * 6 + h1) * 24 + (z2 * 2 + aw) * 6
                    spread[at : at + 6, 0:GROUP] = eb[0, aw, :, off : off + GROUP]
    full = spread[0:288, :]
    high = full.astype(BF)
    rest = full - high.astype(F32)
    mid = rest.astype(BF)
    low = (rest - mid.astype(F32)).astype(BF)
    tgt = target[...]
    for w1 in range(WW):
        hot = onehot_rows(tgt, w1)
        block = dot(high, hot) + (dot(mid, hot) + dot(low, hot))
        for g in range(12):
            wide[pl.ds(g * 12 + w1, 24, stride=WIN), :] = block[g * 24 : g * 24 + 24]
    for aw, out in enumerate((out0, out1)):
        for z2 in range(2):
            keys = slice(z2 * 72, z2 * 72 + 72)
            ok = region_k[aw, keys, :] == region_q[aw]
            tails = []
            for h in range(HEADS):
                at = ((z2 * 2 + aw) * HEADS + h) * WIN
                turned = wide[at : at + WIN, 0:72].T
                out[keys, h * MAIN : (h + 1) * MAIN] = jnp.where(
                    ok[:, 0:MAIN], turned[:, 0:MAIN], NEG_FILL
                )
                tails.append(turned[:, MAIN:WIN])
            tails.append(jnp.zeros((72, SPREAD - HEADS * WIN), F32))
            out[keys, TAILS:SPREAD] = jnp.where(
                ok[:, MAIN:], jnp.concatenate(tails, axis=1), NEG_FILL
            )


def expand(earth_bias, target, region_k, region_q):
    return pl.pallas_call(
        expand_kernel,
        name="expand_bias",
        out_shape=(shape((WIN, SPREAD), F32),) * 2,
        in_specs=[VMEM] * 4,
        out_specs=(VMEM,) * 2,
        scratch_shapes=[pltpu.VMEM((288 + SPARE, KEYS), F32), pltpu.VMEM((25 * WIN, 128), F32)],
        compiler_params=params(16),
        cost_estimate=cost(4 * 10**9, 4 * 1024 * 1024),
    )(earth_bias, target, region_k, region_q)


def windows_kernel(aw, seconds, *refs):
    refs = list(refs)
    take = lambda n: [refs.pop(0) for _ in range(n)]
    f, u, wqkv, wo, bias, inner = take(6)
    if aw == 1:
        lat, diag = take(2)
    if True in seconds:
        lon, edge = take(2)
        (w_in,) = take(1)
    (other,) = take(1) if True in seconds else (None,)
    grads, w_s, gb_s = take(3)
    if aw == 1:
        (lon_back,) = take(1)
    x_s, u_s, i_s, low_s, q_s, k_s, v_s, ga_s, gq_s, gk_s, gv_s, att_s, up_s = take(13)
    if aw == 1:
        g_s, lon_s = take(2)
    w_s[...] = w_in[...] if True in seconds else jnp.zeros_like(w_s)
    gb_s[...] = other[...] if aw == 0 and True in seconds else jnp.zeros_like(gb_s)

    def put(row, pair):
        for value, dst in zip(pair, (x_s, u_s)):
            dst[row : row + value.shape[0], :] = value

    for b in range(2):
        lines = inner[b].astype(F32)
        if True in seconds:
            at_lon, at_edge = lon[b].astype(F32), edge[b].astype(F32)
        for n, second in enumerate(seconds):
            for z in range(2):
                for h in range(6):
                    r = aw * 6 + h
                    row = (n * 2 + b) * WIN + z * 72 + h * 12
                    if r >= 9:
                        line = (diag if z else lat)[b, r - 9].astype(F32)
                        put(row, split(line[12:24] if second else line[0:12]))
                        continue
                    if z:
                        line = split(lines[r * 18 : r * 18 + 18])
                    else:
                        line = [a[b, 1, r + 3].astype(F32)[6:24] for a in (f, u)]
                    if second:
                        put(row, [a[12:18] for a in line])
                        halo = at_edge[r * 6 : r * 6 + 6] if z else at_lon[(r + 15) * 6 : (r + 16) * 6]
                        put(row + 6, split(halo))
                    else:
                        put(row, [a[0:12] for a in line])

    weights = wqkv[...].astype(F32)
    wq, wk, wv = [weights[:, i * C : (i + 1) * C].astype(BF) for i in range(3)]
    tokens = len(seconds) * PAIR
    raw = x_s[0:tokens, :]
    centred = raw - jnp.mean(raw, axis=-1, keepdims=True)
    inv_std = lax.rsqrt(jnp.mean(centred * centred, axis=-1, keepdims=True) + EPS)
    normed = centred * inv_std
    low = normed.astype(BF)
    x_s[0:tokens, :] = normed
    i_s[...] = inv_std
    low_s[...] = low
    q_s[...] = dot(low, wq).astype(BF)
    k_s[...] = dot(low, wk).astype(BF)
    v_s[...] = dot(low, wv).astype(BF)
    up = u_s[0:tokens, :].astype(BF)
    ga_s[...] = dot(up, wo[...], 1, 1).astype(BF)
    att_s[...] = jnp.zeros_like(att_s)
    up_s[...] = jnp.zeros_like(up_s)
    for w in range(2 * len(seconds)):
        up_s[w * KEYS : w * KEYS + WIN, :] = up[w * WIN : (w + 1) * WIN]

    lane = lax.broadcasted_iota(jnp.int32, (1, C), 1)
    picks = [
        jnp.where((lane >= h * HD) & (lane < (h + 1) * HD), 1.0, 0.0).astype(BF)
        for h in range(HEADS)
    ]

    def stack(a):
        pad = jnp.zeros((SPREAD - HEADS * WIN, C), BF)
        mains = [a[0:MAIN] * m for m in picks]
        return jnp.concatenate(mains + [a[MAIN:WIN] * m for m in picks] + [pad], axis=0)

    def per_head(a, probs):
        tails = dot(a, probs[:, TAILS:SPREAD])
        heads = []
        for i in range(HEADS // 2):
            pair = dot(a[2 * i * HD : 2 * (i + 1) * HD], probs[:, 2 * i * MAIN : 2 * (i + 1) * MAIN])
            for n in range(2):
                h = 2 * i + n
                main = pair[n * HD : (n + 1) * HD, n * MAIN : (n + 1) * MAIN]
                tail = tails[h * HD : (h + 1) * HD, h * TAIL : (h + 1) * TAIL]
                heads.append(jnp.concatenate([main, tail], axis=1))
        return jnp.concatenate(heads, axis=0)

    for w in range(2 * len(seconds)):
        rows = slice(w * WIN, (w + 1) * WIN)
        low, q, k, v, ga = low_s[rows, :], q_s[rows, :], k_s[rows, :], v_s[rows, :], ga_s[rows, :]
        qs = stack(q)
        gas = stack(ga)
        scores = dot(k, qs, 1, 1)
        grad_probs = dot(v, gas, 1, 1)
        probs, grads_low = [], []
        for i in range(SPREAD // 128):
            cols = slice(i * 128, (i + 1) * 128)
            s = scores[:, cols] * SCALE + bias[:, cols]
            e = jnp.exp(s - jnp.max(s, axis=0, keepdims=True))
            p = e * (1.0 / jnp.sum(e, axis=0, keepdims=True))
            gp = grad_probs[:, cols]
            gs = p * (gp - jnp.sum(p * gp, axis=0, keepdims=True))
            gb_s[:, cols] += gs
            probs.append(p.astype(BF))
            grads_low.append(gs.astype(BF))
        p = jnp.concatenate(probs, axis=1)
        gs = jnp.concatenate(grads_low, axis=1)
        gv_s[rows, :] = dot(p, gas).astype(BF)
        gk_s[rows, :] = (dot(gs, qs) * SCALE).astype(BF)
        gq_s[rows, :] = (per_head(k.T, gs) * SCALE).T.astype(BF)
        att_s[:, w * KEYS : w * KEYS + WIN] = per_head(v.T, p).astype(BF)

    w_s[3 * C : 4 * C, :] += dot(att_s[...], up_s[...])
    gq, gk, gv = gq_s[...], gk_s[...], gv_s[...]
    low_t = low_s[...].T
    w_s[0:C, :] += dot(low_t, gq)
    w_s[C : 2 * C, :] += dot(low_t, gk)
    w_s[2 * C : 3 * C, :] += dot(low_t, gv)
    gu = dot(gq, wq, 1, 1) + dot(gk, wk, 1, 1) + dot(gv, wv, 1, 1)
    normed = x_s[0:tokens, :]
    centre = jnp.mean(gu, axis=-1, keepdims=True)
    along = jnp.mean(gu * normed, axis=-1, keepdims=True)
    grad = i_s[...] * (gu - centre - normed * along)
    grads[...] = grad.astype(BF)
    if aw == 0:
        return

    g_s[0:PAIR, :] = other[...].astype(F32)
    g_s[PAIR : 2 * PAIR, :] = grad[PAIR : 2 * PAIR]
    for b in range(2):
        for z in range(2):
            for r in range(12):
                row = ((r // 6) * 2 + b) * WIN + z * 72 + (r % 6) * 12
                to = b * WIN + (z * 12 + r) * 6
                lon_s[to : to + 6, :] = g_s[row + 6 : row + 12, :]
    lon_back[...] = join(lon_s[0:WIN, :], lon_s[WIN : 2 * WIN, :]).astype(BF)


def fold_kernel(w_s, gb0, gb1, target, core, keep, send, turned, slab):
    slab[0:768, :] = w_s[:, 0:128].astype(BF)
    slab[768:1152, :] = jnp.concatenate([w_s[0:384, 128:192], w_s[384:768, 128:192]], axis=1).astype(BF)
    for z2 in range(2):
        for aw, gb in enumerate((gb0, gb1)):
            rows = slice(z2 * 72, z2 * 72 + 72)
            tails = gb[rows, TAILS:SPREAD].T
            for h in range(HEADS):
                at = ((z2 * HEADS + h) * 2 + aw) * WIN
                turned[at : at + MAIN, 0:72] = gb[rows, h * MAIN : (h + 1) * MAIN].T
                turned[at + MAIN : at + WIN, 0:72] = tails[h * TAIL : (h + 1) * TAIL]
    folded = jnp.zeros((288, KEYS), F32)
    tgt = target[...]
    for w1 in range(WW):
        rows = [turned[pl.ds(g * 12 + w1, 24, stride=WIN), :] for g in range(12)]
        full = jnp.concatenate(rows, axis=0)[:, 0:72].astype(BF)
        hot = onehot_rows(tgt[:, 0:72], w1)
        folded = folded + dot(full, hot, 1, 1)
    slab[1152:1440, :] = folded[:, 0:128].astype(BF)
    rest = [folded[24 * i : 24 * i + 24, 128:138] for i in range(12)]
    rest = jnp.concatenate(rest + [jnp.zeros((24, 8), F32)], axis=1)
    slab[1440:1536, :] = jnp.concatenate([rest, jnp.zeros((72, 128), F32)], axis=0).astype(BF)
    top = pl.multiple_of(core[0, 0] * SIDE, SIDE)
    keep[...] = slab[pl.ds(top, SIDE), :]
    send[...] = slab[pl.ds(SIDE - top, SIDE), :]


def fold(w, gb0, gb1, target, core):
    return pl.pallas_call(
        fold_kernel,
        name="fold",
        out_shape=(shape((SIDE, 128), BF),) * 2,
        in_specs=[VMEM] * 4 + [SMEM],
        out_specs=(VMEM,) * 2,
        scratch_shapes=[
            pltpu.VMEM((25 * WIN, 128), F32),
            pltpu.VMEM((SLAB, 128), BF),
        ],
        compiler_params=params(24),
        cost_estimate=cost(2 * 10**9, 4 * 1024 * 1024),
    )(w, gb0, gb1, target, core)


def windows(aw, seconds, *args):
    tokens = len(seconds) * PAIR
    padded = 2 * len(seconds) * KEYS
    rows = [pltpu.VMEM((tokens + SPARE, C), F32)] * 2 + [pltpu.VMEM((tokens, 1), F32)]
    rows += [pltpu.VMEM((tokens, C), BF)] * 8
    rows += [pltpu.VMEM((C, padded), BF), pltpu.VMEM((padded, C), BF)]
    outs = (shape((tokens, C), BF), shape((4 * C, C), F32), shape((WIN, SPREAD), F32))
    if aw == 1:
        outs += (shape((WIN, BOTH), BF),)
        rows += [pltpu.VMEM((2 * PAIR + SPARE, C), F32), pltpu.VMEM((2 * WIN + SPARE, C), F32)]
    return pl.pallas_call(
        functools.partial(windows_kernel, aw, seconds),
        name="windows_upper" if aw else "windows_lower_second" if seconds[0] else "windows_lower_first",
        out_shape=outs,
        in_specs=[VMEM] * len(args),
        out_specs=(VMEM,) * len(outs),
        scratch_shapes=rows,
        compiler_params=params(28),
        cost_estimate=cost(3 * 10**9 * len(seconds), 4 * 1024 * 1024),
    )(*args)


def merge_kernel(g_first, g_second, g_upper, lon_in, own, lev, lat, diag):
    halos = split(lon_in[...].astype(F32))
    for aw in range(2):
        first, second = [], []
        for b in range(2):
            at = slice(b * WIN, (b + 1) * WIN)
            after = slice(PAIR + b * WIN, PAIR + (b + 1) * WIN)
            first.append((g_upper if aw else g_first)[at, :].astype(F32))
            second.append((g_upper[after, :] if aw else g_second[at, :]).astype(F32))
        for z in range(2):
            for h in range(6):
                r = aw * 6 + h
                off = z * 72 + h * 12
                hrow = (z * 12 + r) * 6
                lines = [
                    jnp.concatenate(
                        [halos[b][hrow : hrow + 6], first[b][off : off + 12], second[b][off : off + 6]],
                        axis=0,
                    )
                    for b in range(2)
                ]
                if z == 0 and r < 9:
                    for b in range(2):
                        own[b, r] = lines[b].astype(BF)
                    continue
                line = join(*lines).astype(BF)
                if r < 9:
                    lev[r] = line
                else:
                    (diag if z else lat)[r - 9] = line


def merge(*args):
    return pl.pallas_call(
        merge_kernel,
        name="merge_lon",
        out_shape=(
            shape((2, 9, 24, C), BF),
            shape((9, 24, BOTH), BF),
            shape((3, 24, BOTH), BF),
            shape((3, 24, BOTH), BF),
        ),
        in_specs=[VMEM] * 4,
        out_specs=(VMEM,) * 4,
        compiler_params=params(16),
        cost_estimate=cost(2 * 10**10, 2 * 1024 * 1024),
    )(*args)


def place_kernel(own, lev, lat, diag, out):
    for b in range(2):
        out[b, 1, 3:12] = own[b].astype(F32)
    for level, first, rows, src in ((0, 3, 9, lev), (1, 0, 3, lat), (0, 0, 3, diag)):
        for r in range(rows):
            for b, line in enumerate(split(src[r].astype(F32))):
                out[b, level, first + r] = line


def place(own, lev, lat, diag):
    return pl.pallas_call(
        place_kernel,
        name="place_grad",
        out_shape=shape((2, 2, 12, 24, C), F32),
        in_specs=[VMEM] * 4,
        out_specs=VMEM,
        compiler_params=params(16),
        cost_estimate=cost(2 * 10**10, 2 * 1024 * 1024),
    )(own, lev, lat, diag)


def finish_kernel(factor, half, other, core, qkv, out, bias, slab):
    top = pl.multiple_of(core[0, 0] * SIDE, SIDE)
    slab[pl.ds(top, SIDE), :] = half[...].astype(F32)
    slab[pl.ds(SIDE - top, SIDE), :] = other[...].astype(F32)
    full = slab[...]
    right = full[768:1152]
    rest = jnp.concatenate([right[:, 0:64], right[:, 64:128]], axis=0)
    whole = jnp.concatenate([full[0:768], rest], axis=1) * factor
    for j in range(3):
        qkv[:, j * C : (j + 1) * C] = whole[j * C : (j + 1) * C]
    out[...] = whole[3 * C : 4 * C]
    tail = full[1440:1464]
    tail = jnp.concatenate([tail[:, 10 * i : 10 * i + 10] for i in range(12)], axis=0)
    pairs = jnp.concatenate([full[1152:1440], tail], axis=1)
    for z1 in range(2):
        for h1 in range(6):
            for z2 in range(2):
                off = ((z1 * 2 + z2) * 6 + h1) * GROUP
                at = (z1 * 6 + h1) * 24 + z2 * 12
                bias[0, :, :, off : off + GROUP] = pairs[at : at + 12].reshape(HEADS, 2, GROUP)


def finish(half, other, core, factor):
    return pl.pallas_call(
        functools.partial(finish_kernel, factor),
        name="finish_params",
        out_shape=(
            shape((C, 3 * C), F32),
            shape((C, C), F32),
            shape((1, HEADS, 2, PAIRS), F32),
        ),
        in_specs=[VMEM, VMEM, SMEM],
        out_specs=(VMEM,) * 3,
        scratch_shapes=[pltpu.VMEM((SLAB, 128), F32)],
        compiler_params=params(16),
        cost_estimate=cost(0, 2 * 1024 * 1024),
    )(half, other, core)


def from_behind(x, axis, by):
    devices = lax.axis_size(axis)
    return lax.ppermute(x, axis, [(i, (i + by) % devices) for i in range(devices)])


def from_corner(x, by):
    lats, levs = lax.axis_size("lat"), lax.axis_size("lev")
    pairs = [
        (a * levs + v, ((a + by) % lats) * levs + (v + by) % levs)
        for a in range(lats)
        for v in range(levs)
    ]
    return lax.ppermute(x, ("lat", "lev"), pairs)


def other_core(x):
    return lax.ppermute(x, "lon", [(i, i ^ 1) for i in range(lax.axis_size("lon"))])


def reduce_slab(keep, send):
    lons, lats, levs = (lax.axis_size(a) for a in ("lon", "lat", "lev"))
    depth = lons // 4
    rows = SIDE // depth
    along = [[4 * z + low for z in range(depth)] for low in range(4)]
    plane = [
        [((4 * z + 2 * y + c) * lats + a) * levs + v for y in range(2) for a in range(lats) for v in range(levs)]
        for z in range(depth)
        for c in range(2)
    ]
    half = (keep.astype(F32) + other_core(send).astype(F32)).astype(BF)
    pieces = lax.all_to_all(
        half.reshape(depth, rows, 128), "lon", 0, 0, axis_index_groups=along, tiled=True
    )
    mine = jnp.sum(pieces.astype(F32), axis=0).astype(BF)
    count = 2 * lats * levs
    every = lax.all_to_all(
        jnp.broadcast_to(mine[None], (count, rows, 128)),
        ("lon", "lat", "lev"), 0, 0, axis_index_groups=plane, tiled=True,
    )
    lon = lax.axis_index("lon")
    first = (lon % 2) * SIDE + (lon // 4) * rows
    spot = jnp.arange(count, dtype=jnp.int32) % (lats * levs)
    same = spot == lax.axis_index("lat") * levs + lax.axis_index("lev")
    picked = jnp.where(same | (first < WROWS), 1.0, 0.0).astype(F32)
    mine = jnp.sum(every.astype(F32) * picked[:, None, None], axis=0).astype(BF)
    half = lax.all_to_all(
        jnp.broadcast_to(mine[None], (depth, rows, 128)), "lon", 0, 0, axis_index_groups=along, tiled=True
    ).reshape(SIDE, 128)
    return half, other_core(half)


def body(fields, upstream, qkv_weight, out_weight, earth_bias):
    inner = from_behind(pack_lev(fields, upstream), "lev", -1)
    lon = from_behind(pack_lon(fields, upstream), "lon", -1)
    diag_msg, edge_msg, lat_msg = pack_rest(fields, upstream, lon)
    diag = from_corner(diag_msg, -1)
    edge = from_behind(edge_msg, "lev", -1)
    lat = from_behind(lat_msg, "lat", -1)

    key = jnp.arange(WIN, dtype=jnp.int32)
    target = (key // WW) * OFFS - key % WW + WW - 1
    target = target[None, :MAIN]
    last_lev = lax.axis_index("lev") == lax.axis_size("lev") - 1
    last_lat = lax.axis_index("lat") == lax.axis_size("lat") - 1
    lev_flag = ((key // 72) == 1) & last_lev
    lat_flag = ((key // WW) % WH >= WH // 2) & last_lat
    region = jnp.stack(
        [2 * lev_flag.astype(F32), 2 * lev_flag.astype(F32) + lat_flag.astype(F32)]
    )
    ends = jnp.tile(region[:, MAIN:], (1, HEADS))
    pad = jnp.zeros((2, SPREAD - HEADS * WIN), F32)
    along = jnp.concatenate([region[:, :MAIN], ends, pad], axis=1)
    bias0, bias1 = expand(earth_bias, target, region[:, :, None], along[:, None, :])
    core = (lax.axis_index("lon") % 2).astype(jnp.int32).reshape(1, 1)

    shared = (
        fields, upstream,
        qkv_weight, out_weight,
    )
    g_first, w, gb0 = windows(0, (False,), *shared, bias0, inner)
    g_second, w, gb0 = windows(0, (True,), *shared, bias0, inner, lon, edge, w, gb0)
    g_upper, w, gb1, lon_back = windows(
        1, (False, True), *shared, bias1, inner, lat, diag, lon, edge, w, g_second
    )
    keep, send = fold(w, gb0, gb1, target, core)
    half, other = reduce_slab(keep, send)
    lon_in = from_behind(lon_back, "lon", 1)
    own, lev_out, lat_out, diag_out = merge(g_first, g_second, g_upper, lon_in)
    lev_in = from_behind(lev_out, "lev", 1)
    lat_in = from_behind(lat_out, "lat", 1)
    diag_in = from_corner(diag_out, 1)
    field_grad = place(own, lev_in, lat_in, diag_in)

    samples, levels, rows, cols, _ = fields.shape
    tokens = samples * levels * rows * cols
    for axis in ("lon", "lat", "lev"):
        tokens = tokens * lax.axis_size(axis)
    qkv_grad, out_grad, bias_grad = finish(half, other, core, 1.0 / math.sqrt(tokens))
    return (field_grad, qkv_grad, out_grad, bias_grad.transpose(0, 2, 1, 3))


def solution(mesh):
    return jax.shard_map(
        body,
        mesh=mesh,
        in_specs=(
            P(None, "lev", "lat", "lon", None),
            P(None, "lev", "lat", "lon", None),
            P(),
            P(),
            P("lev", "lat", None, None),
        ),
        out_specs=(P(None, "lev", "lat", "lon", None), P(), P(), P("lev", "lat", None, None)),
        check_vma=False,
    )
```

```python
import functools
import math

import jax
import jax.numpy as jnp
from jax import lax
from jax.experimental import pallas as pl
from jax.experimental.pallas import tpu as pltpu
from jax.sharding import PartitionSpec as P

HEADS = 6
WZ = 2
WH = 6
WW = 12
WIN = 144
PAIRS = 3312
C = 192
HD = 32
OFFS = 2 * WW - 1
GROUP = WH * OFFS
LANES = 384
KEYS = 256
SPOTS = 144
NEG_FILL = -1e30
EPS = 1e-05
SCALE = HD**-0.5
SLAB = 1536
SIDE = SLAB // 2
WROWS = 1152
BF = jnp.bfloat16
F32 = jnp.float32
SPREAD = 896
MAIN = 128
TAIL = WIN - MAIN
TAILS = HEADS * MAIN
PAIR = 2 * WIN
BOTH = 2 * C
SPARE = 8
VMEM = pl.BlockSpec(memory_space=pltpu.VMEM)
HBM = pl.BlockSpec(memory_space=pl.ANY)
SMEM = pl.BlockSpec(memory_space=pltpu.SMEM)


def params(mib):
    return pltpu.CompilerParams(vmem_limit_bytes=mib * 1024 * 1024)


def cost(flops, nbytes):
    return pl.CostEstimate(flops=flops, bytes_accessed=nbytes, transcendentals=0)


def dot(a, b, ca=1, cb=0):
    return lax.dot_general(a, b, (((ca,), (cb,)), ((), ())), preferred_element_type=F32)


def shape(dims, dtype):
    return jax.ShapeDtypeStruct(dims, dtype)


def join(a, b):
    return jnp.concatenate([a[:, 0:128], b[:, 0:128], a[:, 128:C], b[:, 128:C]], axis=1)


def split(m):
    return (
        jnp.concatenate([m[:, 0:128], m[:, 256:320]], axis=1),
        jnp.concatenate([m[:, 128:256], m[:, 320:384]], axis=1),
    )


def both_lines(f, u, b, level, row):
    return join(f[b, level, row].astype(F32), u[b, level, row].astype(F32))


def pack_lev_kernel(f, u, out, tmp):
    for b in range(2):
        for r in range(9):
            tmp[b, r * 18 : r * 18 + 18, :] = both_lines(f, u, b, 0, r + 3)[6:24]
    out[...] = tmp[:, 0 : out.shape[1], :].astype(BF)


def pack_lev(fields, upstream):
    return pl.pallas_call(
        pack_lev_kernel,
        name="pack_lev",
        out_shape=shape((2, 162, BOTH), BF),
        in_specs=[VMEM] * 2,
        out_specs=VMEM,
        scratch_shapes=[pltpu.VMEM((2, 168 + SPARE, BOTH), F32)],
        compiler_params=params(16),
        cost_estimate=cost(0, 2 * 1024 * 1024),
    )(fields, upstream)


def pack_lon_kernel(f, u, out, tmp):
    for b in range(2):
        for level in range(2):
            for row in range(12):
                at = (level * 12 + row) * 6
                tmp[b, at : at + 6, :] = both_lines(f, u, b, level, row)[0:6]
    out[...] = tmp[:, 0 : out.shape[1], :].astype(BF)


def pack_lon(fields, upstream):
    return pl.pallas_call(
        pack_lon_kernel,
        name="pack_lon",
        out_shape=shape((2, WIN, BOTH), BF),
        in_specs=[VMEM] * 2,
        out_specs=VMEM,
        scratch_shapes=[pltpu.VMEM((2, WIN + SPARE, BOTH), F32)],
        compiler_params=params(16),
        cost_estimate=cost(0, 2 * 1024 * 1024),
    )(fields, upstream)


def pack_rest_kernel(f, u, lon, diag, edge, lat):
    for b in range(2):
        halo = lon[b].astype(F32)
        for level, out in ((0, diag), (1, lat)):
            for row in range(3):
                at = (level * 12 + row) * 6
                line = both_lines(f, u, b, level, row)
                out[b, row] = jnp.concatenate([line[6:24], halo[at : at + 6]], axis=0).astype(BF)
        edge[b] = halo[18:72].astype(BF)


def pack_rest(fields, upstream, lon):
    return pl.pallas_call(
        pack_rest_kernel,
        name="pack_rest",
        out_shape=(
            shape((2, 3, 24, BOTH), BF), shape((2, 54, BOTH), BF), shape((2, 3, 24, BOTH), BF)
        ),
        in_specs=[VMEM] * 3,
        out_specs=(VMEM,) * 3,
        compiler_params=params(16),
        cost_estimate=cost(0, 2 * 1024 * 1024),
    )(fields, upstream, lon)


def onehot_rows(target, w1):
    row = lax.broadcasted_iota(jnp.int32, (SPOTS, target.shape[1]), 0)
    return jnp.where(row == target + w1, 1.0, 0.0).astype(BF)


def expand_kernel(eb, target, region_k, region_q, out0, out1, spread, wide):
    spread[...] = jnp.zeros_like(spread)
    for z1 in range(2):
        for h1 in range(6):
            for z2 in range(2):
                off = ((z1 * 2 + z2) * 6 + h1) * GROUP
                for aw in range(2):
                    at = (z1 * 6 + h1) * 24 + (z2 * 2 + aw) * 6
                    spread[at : at + 6, 0:GROUP] = eb[0, aw, :, off : off + GROUP]
    full = spread[0:288, :]
    high = full.astype(BF)
    rest = full - high.astype(F32)
    mid = rest.astype(BF)
    low = (rest - mid.astype(F32)).astype(BF)
    tgt = target[...]
    for w1 in range(WW):
        hot = onehot_rows(tgt, w1)
        block = dot(high, hot) + (dot(mid, hot) + dot(low, hot))
        for g in range(12):
            wide[pl.ds(g * 12 + w1, 24, stride=WIN), :] = block[g * 24 : g * 24 + 24]
    for aw, out in enumerate((out0, out1)):
        for z2 in range(2):
            keys = slice(z2 * 72, z2 * 72 + 72)
            ok = region_k[aw, keys, :] == region_q[aw]
            tails = []
            for h in range(HEADS):
                at = ((z2 * 2 + aw) * HEADS + h) * WIN
                turned = wide[at : at + WIN, 0:72].T
                out[keys, h * MAIN : (h + 1) * MAIN] = jnp.where(
                    ok[:, 0:MAIN], turned[:, 0:MAIN], NEG_FILL
                )
                tails.append(turned[:, MAIN:WIN])
            tails.append(jnp.zeros((72, SPREAD - HEADS * WIN), F32))
            out[keys, TAILS:SPREAD] = jnp.where(
                ok[:, MAIN:], jnp.concatenate(tails, axis=1), NEG_FILL
            )


def expand(earth_bias, target, region_k, region_q):
    return pl.pallas_call(
        expand_kernel,
        name="expand_bias",
        out_shape=(shape((WIN, SPREAD), F32),) * 2,
        in_specs=[VMEM] * 4,
        out_specs=(VMEM,) * 2,
        scratch_shapes=[pltpu.VMEM((288 + SPARE, SPOTS), F32), pltpu.VMEM((25 * WIN, 128), F32)],
        compiler_params=params(16),
        cost_estimate=cost(4 * 10**9, 4 * 1024 * 1024),
    )(earth_bias, target, region_k, region_q)


def windows_kernel(aw, seconds, *refs):
    refs = list(refs)
    take = lambda n: [refs.pop(0) for _ in range(n)]
    f, u, wqkv, wo, bias, inner = take(6)
    if aw == 1:
        lat, diag = take(2)
    if True in seconds:
        lon, edge = take(2)
        (w_in,) = take(1)
    (other,) = take(1) if True in seconds else (None,)
    grads, w_s, gb_s = take(3)
    if aw == 1:
        (lon_back,) = take(1)
    x_s, u_s, i_s, low_s, q_s, k_s, v_s, ga_s, gq_s, gk_s, gv_s, att_s, up_s = take(13)
    if aw == 1:
        g_s, lon_s = take(2)
    w_s[...] = w_in[...] if True in seconds else jnp.zeros_like(w_s)
    gb_s[...] = other[...] if aw == 0 and True in seconds else jnp.zeros_like(gb_s)

    def put(row, pair):
        for value, dst in zip(pair, (x_s, u_s)):
            dst[row : row + value.shape[0], :] = value

    for b in range(2):
        lines = inner[b].astype(F32)
        if True in seconds:
            at_lon, at_edge = lon[b].astype(F32), edge[b].astype(F32)
        for n, second in enumerate(seconds):
            for z in range(2):
                for h in range(6):
                    r = aw * 6 + h
                    row = (n * 2 + b) * WIN + z * 72 + h * 12
                    if r >= 9:
                        line = (diag if z else lat)[b, r - 9].astype(F32)
                        put(row, split(line[12:24] if second else line[0:12]))
                        continue
                    if z:
                        line = split(lines[r * 18 : r * 18 + 18])
                    else:
                        line = [a[b, 1, r + 3].astype(F32)[6:24] for a in (f, u)]
                    if second:
                        put(row, [a[12:18] for a in line])
                        halo = at_edge[r * 6 : r * 6 + 6] if z else at_lon[(r + 15) * 6 : (r + 16) * 6]
                        put(row + 6, split(halo))
                    else:
                        put(row, [a[0:12] for a in line])

    weights = wqkv[...].astype(F32)
    wq, wk, wv = [weights[:, i * C : (i + 1) * C].astype(BF) for i in range(3)]
    tokens = len(seconds) * PAIR
    raw = x_s[0:tokens, :]
    centred = raw - jnp.mean(raw, axis=-1, keepdims=True)
    inv_std = lax.rsqrt(jnp.mean(centred * centred, axis=-1, keepdims=True) + EPS)
    normed = centred * inv_std
    low = normed.astype(BF)
    x_s[0:tokens, :] = normed
    i_s[...] = inv_std
    low_s[...] = low
    q_s[...] = dot(low, wq).astype(BF)
    k_s[...] = dot(low, wk).astype(BF)
    v_s[...] = dot(low, wv).astype(BF)
    up = u_s[0:tokens, :].astype(BF)
    ga_s[...] = dot(up, wo[...], 1, 1).astype(BF)
    att_s[...] = jnp.zeros_like(att_s)
    up_s[...] = jnp.zeros_like(up_s)
    for w in range(2 * len(seconds)):
        up_s[w * KEYS : w * KEYS + WIN, :] = up[w * WIN : (w + 1) * WIN]

    lane = lax.broadcasted_iota(jnp.int32, (1, C), 1)
    picks = [
        jnp.where((lane >= h * HD) & (lane < (h + 1) * HD), 1.0, 0.0).astype(BF)
        for h in range(HEADS)
    ]

    def stack(a):
        pad = jnp.zeros((SPREAD - HEADS * WIN, C), BF)
        mains = [a[0:MAIN] * m for m in picks]
        return jnp.concatenate(mains + [a[MAIN:WIN] * m for m in picks] + [pad], axis=0)

    def per_head(a, probs):
        tails = dot(a, probs[:, TAILS:SPREAD])
        heads = []
        for i in range(HEADS // 2):
            pair = dot(a[2 * i * HD : 2 * (i + 1) * HD], probs[:, 2 * i * MAIN : 2 * (i + 1) * MAIN])
            for n in range(2):
                h = 2 * i + n
                main = pair[n * HD : (n + 1) * HD, n * MAIN : (n + 1) * MAIN]
                tail = tails[h * HD : (h + 1) * HD, h * TAIL : (h + 1) * TAIL]
                heads.append(jnp.concatenate([main, tail], axis=1))
        return jnp.concatenate(heads, axis=0)

    for w in range(2 * len(seconds)):
        rows = slice(w * WIN, (w + 1) * WIN)
        low, q, k, v, ga = low_s[rows, :], q_s[rows, :], k_s[rows, :], v_s[rows, :], ga_s[rows, :]
        qs = stack(q)
        gas = stack(ga)
        scores = dot(k, qs, 1, 1)
        grad_probs = dot(v, gas, 1, 1)
        probs, grads_low = [], []
        for i in range(SPREAD // 128):
            cols = slice(i * 128, (i + 1) * 128)
            s = scores[:, cols] * SCALE + bias[:, cols]
            e = jnp.exp(s - jnp.max(s, axis=0, keepdims=True))
            p = e * (1.0 / jnp.sum(e, axis=0, keepdims=True))
            gp = grad_probs[:, cols]
            gs = p * (gp - jnp.sum(p * gp, axis=0, keepdims=True))
            gb_s[:, cols] += gs
            probs.append(p.astype(BF))
            grads_low.append(gs.astype(BF))
        p = jnp.concatenate(probs, axis=1)
        gs = jnp.concatenate(grads_low, axis=1)
        gv_s[rows, :] = dot(p, gas).astype(BF)
        gk_s[rows, :] = (dot(gs, qs) * SCALE).astype(BF)
        gq_s[rows, :] = (per_head(k.T, gs) * SCALE).T.astype(BF)
        att_s[:, w * KEYS : w * KEYS + WIN] = per_head(v.T, p).astype(BF)

    w_s[3 * C : 4 * C, :] += dot(att_s[...], up_s[...])
    gq, gk, gv = gq_s[...], gk_s[...], gv_s[...]
    low_t = low_s[...].T
    w_s[0:C, :] += dot(low_t, gq)
    w_s[C : 2 * C, :] += dot(low_t, gk)
    w_s[2 * C : 3 * C, :] += dot(low_t, gv)
    gu = dot(gq, wq, 1, 1) + dot(gk, wk, 1, 1) + dot(gv, wv, 1, 1)
    normed = x_s[0:tokens, :]
    centre = jnp.mean(gu, axis=-1, keepdims=True)
    along = jnp.mean(gu * normed, axis=-1, keepdims=True)
    grad = i_s[...] * (gu - centre - normed * along)
    grads[...] = grad.astype(BF)
    if aw == 0:
        return

    g_s[0:PAIR, :] = other[...].astype(F32)
    g_s[PAIR : 2 * PAIR, :] = grad[PAIR : 2 * PAIR]
    for b in range(2):
        for z in range(2):
            for r in range(12):
                row = ((r // 6) * 2 + b) * WIN + z * 72 + (r % 6) * 12
                to = b * WIN + (z * 12 + r) * 6
                lon_s[to : to + 6, :] = g_s[row + 6 : row + 12, :]
    lon_back[...] = join(lon_s[0:WIN, :], lon_s[WIN : 2 * WIN, :]).astype(BF)


def fold_kernel(w_s, gb0, gb1, target, core, keep, send, turned, slab):
    slab[0:768, :] = w_s[:, 0:128].astype(BF)
    slab[768:1152, :] = jnp.concatenate([w_s[0:384, 128:192], w_s[384:768, 128:192]], axis=1).astype(BF)
    for z2 in range(2):
        for aw, gb in enumerate((gb0, gb1)):
            rows = slice(z2 * 72, z2 * 72 + 72)
            tails = gb[rows, TAILS:SPREAD].T
            for h in range(HEADS):
                at = ((z2 * HEADS + h) * 2 + aw) * WIN
                turned[at : at + MAIN, 0:72] = gb[rows, h * MAIN : (h + 1) * MAIN].T
                turned[at + MAIN : at + WIN, 0:72] = tails[h * TAIL : (h + 1) * TAIL]
    folded = jnp.zeros((288, SPOTS), F32)
    tgt = target[...]
    for w1 in range(WW):
        rows = [turned[pl.ds(g * 12 + w1, 24, stride=WIN), :] for g in range(12)]
        full = jnp.concatenate(rows, axis=0)[:, 0:72].astype(BF)
        hot = onehot_rows(tgt[:, 0:72], w1)
        folded = folded + dot(full, hot, 1, 1)
    slab[1152:1440, :] = folded[:, 0:128].astype(BF)
    rest = [folded[24 * i : 24 * i + 24, 128:138] for i in range(12)]
    rest = jnp.concatenate(rest + [jnp.zeros((24, 8), F32)], axis=1)
    slab[1440:1536, :] = jnp.concatenate([rest, jnp.zeros((72, 128), F32)], axis=0).astype(BF)
    top = pl.multiple_of(core[0, 0] * SIDE, SIDE)
    keep[...] = slab[pl.ds(top, SIDE), :]
    send[...] = slab[pl.ds(SIDE - top, SIDE), :]


def fold(w, gb0, gb1, target, core):
    return pl.pallas_call(
        fold_kernel,
        name="fold",
        out_shape=(shape((SIDE, 128), BF),) * 2,
        in_specs=[VMEM] * 4 + [SMEM],
        out_specs=(VMEM,) * 2,
        scratch_shapes=[
            pltpu.VMEM((25 * WIN, 128), F32),
            pltpu.VMEM((SLAB, 128), BF),
        ],
        compiler_params=params(24),
        cost_estimate=cost(2 * 10**9, 4 * 1024 * 1024),
    )(w, gb0, gb1, target, core)


def windows(aw, seconds, *args):
    tokens = len(seconds) * PAIR
    padded = 2 * len(seconds) * KEYS
    rows = [pltpu.VMEM((tokens + SPARE, C), F32)] * 2 + [pltpu.VMEM((tokens, 1), F32)]
    rows += [pltpu.VMEM((tokens, C), BF)] * 8
    rows += [pltpu.VMEM((C, padded), BF), pltpu.VMEM((padded, C), BF)]
    outs = (shape((tokens, C), BF), shape((4 * C, C), F32), shape((WIN, SPREAD), F32))
    if aw == 1:
        outs += (shape((WIN, BOTH), BF),)
        rows += [pltpu.VMEM((2 * PAIR + SPARE, C), F32), pltpu.VMEM((2 * WIN + SPARE, C), F32)]
    return pl.pallas_call(
        functools.partial(windows_kernel, aw, seconds),
        name="windows_upper" if aw else "windows_lower_second" if seconds[0] else "windows_lower_first",
        out_shape=outs,
        in_specs=[VMEM] * len(args),
        out_specs=(VMEM,) * len(outs),
        scratch_shapes=rows,
        compiler_params=params(28),
        cost_estimate=cost(3 * 10**9 * len(seconds), 4 * 1024 * 1024),
    )(*args)


def merge_kernel(g_first, g_second, g_upper, lon_in, own, lev, lat, diag):
    halos = split(lon_in[...].astype(F32))
    for aw in range(2):
        first, second = [], []
        for b in range(2):
            at = slice(b * WIN, (b + 1) * WIN)
            after = slice(PAIR + b * WIN, PAIR + (b + 1) * WIN)
            first.append((g_upper if aw else g_first)[at, :].astype(F32))
            second.append((g_upper[after, :] if aw else g_second[at, :]).astype(F32))
        for z in range(2):
            for h in range(6):
                r = aw * 6 + h
                off = z * 72 + h * 12
                hrow = (z * 12 + r) * 6
                lines = [
                    jnp.concatenate(
                        [halos[b][hrow : hrow + 6], first[b][off : off + 12], second[b][off : off + 6]],
                        axis=0,
                    )
                    for b in range(2)
                ]
                if z == 0 and r < 9:
                    for b in range(2):
                        own[b, r] = lines[b].astype(BF)
                    continue
                line = join(*lines).astype(BF)
                if r < 9:
                    lev[r] = line
                else:
                    (diag if z else lat)[r - 9] = line


def merge(*args):
    return pl.pallas_call(
        merge_kernel,
        name="merge_lon",
        out_shape=(
            shape((2, 9, 24, C), BF),
            shape((9, 24, BOTH), BF),
            shape((3, 24, BOTH), BF),
            shape((3, 24, BOTH), BF),
        ),
        in_specs=[VMEM] * 4,
        out_specs=(VMEM,) * 4,
        compiler_params=params(16),
        cost_estimate=cost(2 * 10**10, 2 * 1024 * 1024),
    )(*args)


def place_kernel(own, lev, lat, diag, out):
    for b in range(2):
        out[b, 1, 3:12] = own[b].astype(F32)
    for level, first, rows, src in ((0, 3, 9, lev), (1, 0, 3, lat), (0, 0, 3, diag)):
        for r in range(rows):
            for b, line in enumerate(split(src[r].astype(F32))):
                out[b, level, first + r] = line


def place(own, lev, lat, diag):
    return pl.pallas_call(
        place_kernel,
        name="place_grad",
        out_shape=shape((2, 2, 12, 24, C), F32),
        in_specs=[VMEM] * 4,
        out_specs=VMEM,
        compiler_params=params(16),
        cost_estimate=cost(2 * 10**10, 2 * 1024 * 1024),
    )(own, lev, lat, diag)


def finish_kernel(factor, half, other, core, qkv, out, bias, slab):
    top = pl.multiple_of(core[0, 0] * SIDE, SIDE)
    slab[pl.ds(top, SIDE), :] = half[...].astype(F32)
    slab[pl.ds(SIDE - top, SIDE), :] = other[...].astype(F32)
    full = slab[...]
    right = full[768:1152]
    rest = jnp.concatenate([right[:, 0:64], right[:, 64:128]], axis=0)
    whole = jnp.concatenate([full[0:768], rest], axis=1) * factor
    for j in range(3):
        qkv[:, j * C : (j + 1) * C] = whole[j * C : (j + 1) * C]
    out[...] = whole[3 * C : 4 * C]
    tail = full[1440:1464]
    tail = jnp.concatenate([tail[:, 10 * i : 10 * i + 10] for i in range(12)], axis=0)
    pairs = jnp.concatenate([full[1152:1440], tail], axis=1)
    for z1 in range(2):
        for h1 in range(6):
            for z2 in range(2):
                off = ((z1 * 2 + z2) * 6 + h1) * GROUP
                at = (z1 * 6 + h1) * 24 + z2 * 12
                bias[0, :, :, off : off + GROUP] = pairs[at : at + 12].reshape(HEADS, 2, GROUP)


def finish(half, other, core, factor):
    return pl.pallas_call(
        functools.partial(finish_kernel, factor),
        name="finish_params",
        out_shape=(
            shape((C, 3 * C), F32),
            shape((C, C), F32),
            shape((1, HEADS, 2, PAIRS), F32),
        ),
        in_specs=[VMEM, VMEM, SMEM],
        out_specs=(VMEM,) * 3,
        scratch_shapes=[pltpu.VMEM((SLAB, 128), F32)],
        compiler_params=params(16),
        cost_estimate=cost(0, 2 * 1024 * 1024),
    )(half, other, core)


def from_behind(x, axis, by):
    devices = lax.axis_size(axis)
    return lax.ppermute(x, axis, [(i, (i + by) % devices) for i in range(devices)])


def from_corner(x, by):
    lats, levs = lax.axis_size("lat"), lax.axis_size("lev")
    pairs = [
        (a * levs + v, ((a + by) % lats) * levs + (v + by) % levs)
        for a in range(lats)
        for v in range(levs)
    ]
    return lax.ppermute(x, ("lat", "lev"), pairs)


def other_core(x):
    return lax.ppermute(x, "lon", [(i, i ^ 1) for i in range(lax.axis_size("lon"))])


def reduce_slab(keep, send):
    lons, lats, levs = (lax.axis_size(a) for a in ("lon", "lat", "lev"))
    depth = lons // 4
    rows = SIDE // depth
    along = [[4 * z + low for z in range(depth)] for low in range(4)]
    plane = [
        [((4 * z + 2 * y + c) * lats + a) * levs + v for y in range(2) for a in range(lats) for v in range(levs)]
        for z in range(depth)
        for c in range(2)
    ]
    half = (keep.astype(F32) + other_core(send).astype(F32)).astype(BF)
    pieces = lax.all_to_all(
        half.reshape(depth, rows, 128), "lon", 0, 0, axis_index_groups=along, tiled=True
    )
    mine = jnp.sum(pieces.astype(F32), axis=0).astype(BF)
    count = 2 * lats * levs
    every = lax.all_to_all(
        jnp.broadcast_to(mine[None], (count, rows, 128)),
        ("lon", "lat", "lev"), 0, 0, axis_index_groups=plane, tiled=True,
    )
    lon = lax.axis_index("lon")
    first = (lon % 2) * SIDE + (lon // 4) * rows
    spot = jnp.arange(count, dtype=jnp.int32) % (lats * levs)
    same = spot == lax.axis_index("lat") * levs + lax.axis_index("lev")
    picked = jnp.where(same | (first < WROWS), 1.0, 0.0).astype(F32)
    mine = jnp.sum(every.astype(F32) * picked[:, None, None], axis=0).astype(BF)
    half = lax.all_to_all(
        jnp.broadcast_to(mine[None], (depth, rows, 128)), "lon", 0, 0, axis_index_groups=along, tiled=True
    ).reshape(SIDE, 128)
    return half, other_core(half)


def body(fields, upstream, qkv_weight, out_weight, earth_bias):
    inner = from_behind(pack_lev(fields, upstream), "lev", -1)
    lon = from_behind(pack_lon(fields, upstream), "lon", -1)
    diag_msg, edge_msg, lat_msg = pack_rest(fields, upstream, lon)
    diag = from_corner(diag_msg, -1)
    edge = from_behind(edge_msg, "lev", -1)
    lat = from_behind(lat_msg, "lat", -1)

    key = jnp.arange(WIN, dtype=jnp.int32)
    target = (key // WW) * OFFS - key % WW + WW - 1
    target = target[None, :MAIN]
    last_lev = lax.axis_index("lev") == lax.axis_size("lev") - 1
    last_lat = lax.axis_index("lat") == lax.axis_size("lat") - 1
    lev_flag = ((key // 72) == 1) & last_lev
    lat_flag = ((key // WW) % WH >= WH // 2) & last_lat
    region = jnp.stack(
        [2 * lev_flag.astype(F32), 2 * lev_flag.astype(F32) + lat_flag.astype(F32)]
    )
    ends = jnp.tile(region[:, MAIN:], (1, HEADS))
    pad = jnp.zeros((2, SPREAD - HEADS * WIN), F32)
    along = jnp.concatenate([region[:, :MAIN], ends, pad], axis=1)
    bias0, bias1 = expand(earth_bias, target, region[:, :, None], along[:, None, :])
    core = (lax.axis_index("lon") % 2).astype(jnp.int32).reshape(1, 1)

    shared = (
        fields, upstream,
        qkv_weight, out_weight,
    )
    g_first, w, gb0 = windows(0, (False,), *shared, bias0, inner)
    g_second, w, gb0 = windows(0, (True,), *shared, bias0, inner, lon, edge, w, gb0)
    g_upper, w, gb1, lon_back = windows(
        1, (False, True), *shared, bias1, inner, lat, diag, lon, edge, w, g_second
    )
    keep, send = fold(w, gb0, gb1, target, core)
    half, other = reduce_slab(keep, send)
    lon_in = from_behind(lon_back, "lon", 1)
    own, lev_out, lat_out, diag_out = merge(g_first, g_second, g_upper, lon_in)
    lev_in = from_behind(lev_out, "lev", 1)
    lat_in = from_behind(lat_out, "lat", 1)
    diag_in = from_corner(diag_out, 1)
    field_grad = place(own, lev_in, lat_in, diag_in)

    samples, levels, rows, cols, _ = fields.shape
    tokens = samples * levels * rows * cols
    for axis in ("lon", "lat", "lev"):
        tokens = tokens * lax.axis_size(axis)
    qkv_grad, out_grad, bias_grad = finish(half, other, core, 1.0 / math.sqrt(tokens))
    return (field_grad, qkv_grad, out_grad, bias_grad.transpose(0, 2, 1, 3))


def solution(mesh):
    return jax.shard_map(
        body,
        mesh=mesh,
        in_specs=(
            P(None, "lev", "lat", "lon", None),
            P(None, "lev", "lat", "lon", None),
            P(),
            P(),
            P("lev", "lat", None, None),
        ),
        out_specs=(P(None, "lev", "lat", "lon", None), P(), P(), P("lev", "lat", None, None)),
        check_vma=False,
    )
```
